32 devices in a mesh: abl: 2 (over y), head: 4 (over x, core), ctx: 4 (over z).
Axes of the slice: x: 2, y: 2, z: 4, core: 2. Of those that a mesh axis runs over, the one named last changes fastest.
Arguments:
- queries: bfloat16 [1024, 6144], P(('abl', 'head', 'ctx')), parts along dimension 0, may hold values from -30 to 30
- keys: bfloat16 [16384, 6144], P(('abl', 'ctx'), 'head'), parts along dimension 0, may hold values from -6 to 6
- values: bfloat16 [16384, 6144], P(('abl', 'ctx'), 'head'), parts along dimension 0, may hold values from -6 to 6
- kept_rows: int32 [128], P(('abl', 'ctx')), parts along dimension 0, may hold values from 0 to 1, as said below
- out_weight: bfloat16 [6144, 6144], P('head'), may hold values from -6 to 6
Outputs:
- projected: bfloat16 [1024, 6144], P(('abl', 'head', 'ctx')), parts along dimension 0
The draws below stay inside these ranges and needn't reach their ends.
There are 2 independent parts, one for each index of `abl`. The reference program is written for one: setup_inputs(seed, part) draws one part's arguments, and reference() takes and returns one part's arrays. A program takes and returns all parts, laid end to end along the dimension named above; an argument that names none is the same for every part. Nothing has to cross between parts.
Inputs may be any that keep to these rules, and one draw needn't show every extreme that they name: `kept_rows`: in every part the first row of each block of 16 consecutive rows is kept.
All inputs are finite; a program needn't handle non-finite values.
Results may differ from the reference program's by a relative error of at most 0.028.
Values may be sent and summed in bfloat16 or wider, within the bound.
A program may use at most 128 MiB of HBM per device.

```python
import math
import jax
import jax.numpy as jnp
from jax import lax

HEADS = 48
HD = 128
Q_TOK = 512
KV_DEV = 2048
KEPT = 8192
N_CTX = 4


def joint_draw(key):
    key_query, key_key = jax.random.split(key, 2)
    width = HEADS * HD
    query_draw = jnp.clip(jax.random.normal(key_query, (Q_TOK, width), jnp.float32), -6.0, 6.0)
    key_draw = jnp.clip(jax.random.normal(key_key, (KEPT, width), jnp.float32), -6.0, 6.0)
    return (query_draw, key_draw)


def draw_queries(key, part):
    return joint_draw(jax.random.fold_in(key, 7))[0].astype(jnp.bfloat16)


def draw_keys(key, part):
    return joint_draw(jax.random.fold_in(key, 7))[1].astype(jnp.bfloat16)


def draw_kept_rows(key, part):
    row_total = KEPT // 128
    block_rows = KV_DEV // 128
    key_flags, key_block, key_offset = jax.random.split(key, 3)
    flags = (jax.random.randint(key_flags, (row_total,), 0, 4) > 0).astype(jnp.int32)
    position = jnp.arange(row_total)
    dropped_block = jax.random.randint(key_block, (), 0, row_total // block_rows)
    dropped_offset = jax.random.randint(key_offset, (), 1, block_rows)
    dropped = dropped_block * block_rows + dropped_offset
    flags = jnp.where(position == dropped, 0, flags)
    return jnp.where(position % block_rows == 0, 1, flags).astype(jnp.int32)


def shard_levels(stream_key, dims, pieces, least, largest):
    def one(dim, parts):
        heights = jax.random.uniform(jax.random.fold_in(jax.random.fold_in(stream_key, 6), dim), (parts,), jnp.float32, least / len(pieces), largest / len(pieces))
        return jnp.repeat(jnp.exp(heights), dims[dim] // parts).reshape((-1,) + (1,) * (len(dims) - dim - 1))

    loudness = one(*pieces[0])
    for cut in pieces[1:]:
        loudness = loudness * one(*cut)
    return loudness


def gaussian(own_key, dims, deviation, limit, pieces=(), dtype=jnp.bfloat16):
    level = shard_levels(own_key, dims, pieces, -0.22, 0.18) if pieces else 1.0
    array = jax.random.normal(own_key, dims, jnp.float32) * deviation * level
    return jnp.minimum(jnp.maximum(array, -limit), limit).astype(dtype)


def setup_inputs(seed: int = 0, part: int = 0) -> dict:
    key_of = jax.random.split(jax.random.key(seed), 6)
    part_splits = jax.random.split(jax.random.fold_in(key_of[5], part), 6)
    return {
        "queries": draw_queries(jax.random.fold_in(jax.random.fold_in(key_of[5], part), 71), part),
        "keys": draw_keys(jax.random.fold_in(jax.random.fold_in(key_of[5], part), 71), part),
        "values": gaussian(part_splits[2], (KEPT, HEADS * HD), 1.0, 6.0, ((0, 4), (1, 4))),
        "kept_rows": draw_kept_rows(jax.random.fold_in(jax.random.fold_in(key_of[5], part), 71), part),
        "out_weight": gaussian(key_of[4], (HEADS * HD, HEADS * HD), (max(1, HEADS * HD // KEPT)) ** -0.5, 6.0, ((0, 4),)),
    }


def reference(queries, keys, values, kept_rows, out_weight):
    score_scale = 1.0 / math.sqrt(HD)
    query_heads = queries.reshape(Q_TOK, HEADS, HD).astype(jnp.float32)
    key_blocks = keys.reshape(N_CTX, KV_DEV, HEADS, HD)
    value_blocks = values.reshape(N_CTX, KV_DEV, HEADS, HD)
    visible = (jnp.repeat(kept_rows, 128) > 0).reshape(N_CTX, KV_DEV)

    def absorb(carry, block):
        summed, running, normal_sum = carry
        key_block, value_block, seen = block
        scores = jnp.einsum('qhd,khd->hqk', query_heads, key_block.astype(jnp.float32)) * score_scale
        scores = jnp.where(seen[None, None, :], scores, -jnp.inf)
        highest = jnp.maximum(running, lax.optimization_barrier(jnp.max(scores, axis=-1)))
        rescale = jnp.exp(running - highest)
        softened = jnp.exp(scores - highest[..., None])
        normal_sum = normal_sum * rescale + lax.optimization_barrier(jnp.sum(softened, axis=-1))
        rounded = softened.astype(jnp.bfloat16).astype(jnp.float32)
        mixed = jnp.einsum('hqk,khd->hqd', rounded, value_block.astype(jnp.float32))
        summed = summed * rescale[..., None] + mixed
        return ((summed, highest, normal_sum), None)
    starting = (jnp.zeros((HEADS, Q_TOK, HD), jnp.float32), jnp.full((HEADS, Q_TOK), -1e+30, jnp.float32), jnp.zeros((HEADS, Q_TOK), jnp.float32))
    finished, _ = lax.scan(absorb, starting, (key_blocks, value_blocks, visible))
    summed, running, normal_sum = finished
    attended = (summed / normal_sum[..., None]).transpose(1, 0, 2).reshape(Q_TOK, HEADS * HD).astype(jnp.bfloat16)
    return jnp.dot(attended, out_weight, preferred_element_type=jnp.float32).astype(jnp.bfloat16)
```

```python
import functools
import math

import jax
import jax.numpy as jnp
from jax import lax
from jax.experimental import pallas as pl
from jax.experimental.pallas import tpu as pltpu
from jax.sharding import PartitionSpec as P

HD = 128
MESH = pl.DeviceIdType.MESH
SCALE2 = math.log2(math.e) / math.sqrt(HD)


def general_shards(queries, keys, values, kept_rows, out_weight):
    score_scale = 1.0 / math.sqrt(HD)
    local_heads = keys.shape[1] // HD
    key_count = keys.shape[0]
    key_heads = keys.reshape(key_count, local_heads, HD)
    value_heads = values.reshape(key_count, local_heads, HD)
    visible = jnp.repeat(kept_rows, 128) > 0
    query_block = lax.all_to_all(queries, "head", split_axis=1, concat_axis=0, tiled=True)
    all_queries = lax.all_gather(query_block, "ctx", axis=0, tiled=True)
    row_count = all_queries.shape[0]
    shaped = all_queries.reshape(row_count, local_heads, HD)
    scores = (
        jnp.einsum("qhd,khd->hqk", shaped, key_heads, preferred_element_type=jnp.float32)
        * score_scale
    )
    scores = jnp.where(visible[None, None, :], scores, -jnp.inf)
    running = jnp.max(scores, axis=-1)
    softened = jnp.exp(scores - running[..., None])
    normal_sum = jnp.sum(softened, axis=-1)
    mixed = jnp.einsum(
        "hqk,khd->qhd",
        softened.astype(jnp.bfloat16),
        value_heads,
        preferred_element_type=jnp.float32,
    )
    summed = mixed.reshape(row_count, local_heads * HD)
    highest = lax.pmax(running, "ctx")
    rescale = jnp.exp(running - highest)
    summed = summed * jnp.repeat(rescale.T, HD, axis=1)
    normal_sum = normal_sum * rescale
    summed, normal_sum = (
        lax.psum_scatter(
            summed.astype(jnp.bfloat16), "ctx", scatter_dimension=0, tiled=True
        ).astype(jnp.float32),
        lax.psum_scatter(
            normal_sum.astype(jnp.bfloat16), "ctx", scatter_dimension=1, tiled=True
        ).astype(jnp.float32),
    )
    attended = (summed / jnp.repeat(normal_sum.T, HD, axis=1)).astype(jnp.bfloat16)
    return lax.psum_scatter(
        jnp.dot(attended, out_weight, preferred_element_type=jnp.float32).astype(jnp.bfloat16),
        "head",
        scatter_dimension=0,
        tiled=True,
    )


def kernel(
    q_ref, k_hbm, v_hbm, kept_ref, w_hbm, out_ref,
    kbuf, vbuf, wbuf, qbuf, abuf, sbuf, rbuf, srbuf, bias, att, pbuf, sib, xsend, xrecv,
    kv_sem, w_sem, a2a_s, a2a_r, ag_s, ag_r, rs_s, rs_r, st_s, st_r, sib_s, sib_r, x_s, x_r,
):
    heads, ctxs = 4, qbuf.shape[1]
    groups, _, block, cw = qbuf.shape
    rows = q_ref.shape[0]
    hg = groups * cw
    per = cw // HD
    ncols, _, _, nw = pbuf.shape
    h = lax.axis_index("head")
    c = lax.axis_index("ctx")

    def kv_copies(g):
        cols = pl.ds(pl.multiple_of(g * cw, cw), cw)
        return (
            pltpu.make_async_copy(k_hbm.at[:, cols], kbuf.at[g], kv_sem.at[0, g]),
            pltpu.make_async_copy(v_hbm.at[:, cols], vbuf.at[g], kv_sem.at[1, g]),
        )

    def w_copy(n):
        cols = pl.ds(pl.multiple_of(n * nw, nw), nw)
        return pltpu.make_async_copy(w_hbm.at[:, cols], wbuf.at[n], w_sem.at[n])

    def a2a(g, d, sender, target):
        return pltpu.make_async_remote_copy(
            src_ref=q_ref.at[:, pl.ds(pl.multiple_of(target * hg + g * cw, cw), cw)],
            dst_ref=qbuf.at[g, c, pl.ds(pl.multiple_of(sender * rows, rows), rows), :],
            send_sem=a2a_s.at[g, d - 1], recv_sem=a2a_r.at[g, d - 1],
            device_id={"head": target}, device_id_type=MESH)

    def gather(g, d, sender, target):
        return pltpu.make_async_remote_copy(
            src_ref=qbuf.at[g, sender], dst_ref=qbuf.at[g, sender],
            send_sem=ag_s.at[g, d - 1], recv_sem=ag_r.at[g, d - 1],
            device_id={"ctx": target}, device_id_type=MESH)

    def scatter(g, d, target):
        return (
            pltpu.make_async_remote_copy(
                src_ref=abuf.at[g, target], dst_ref=rbuf.at[g, d - 1],
                send_sem=rs_s.at[g, d - 1], recv_sem=rs_r.at[g, d - 1],
                device_id={"ctx": target}, device_id_type=MESH),
            pltpu.make_async_remote_copy(
                src_ref=sbuf.at[g, target], dst_ref=srbuf.at[g, d - 1],
                send_sem=st_s.at[g, d - 1], recv_sem=st_r.at[g, d - 1],
                device_id={"ctx": target}, device_id_type=MESH),
        )

    sibling = h + 1 - 2 * lax.rem(h, 2)
    across = lax.rem(h + 2, 4)
    diagonal = lax.rem(sibling + 2, 4)

    def to_sibling(n, i):
        return pltpu.make_async_remote_copy(
            src_ref=pbuf.at[n, sibling if i else diagonal], dst_ref=sib.at[n, i],
            send_sem=sib_s.at[n, i], recv_sem=sib_r.at[n, i],
            device_id={"head": sibling}, device_id_type=MESH)

    def to_across(n):
        return pltpu.make_async_remote_copy(
            src_ref=xsend.at[n], dst_ref=xrecv.at[n],
            send_sem=x_s.at[n], recv_sem=x_r.at[n],
            device_id={"head": across}, device_id_type=MESH)

    barrier = pltpu.get_barrier_semaphore()
    for d in range(1, heads):
        pl.semaphore_signal(barrier, inc=1, device_id={"head": lax.rem(h + d, heads)}, device_id_type=MESH)
    for d in range(1, ctxs):
        pl.semaphore_signal(barrier, inc=1, device_id={"ctx": lax.rem(c + d, ctxs)}, device_id_type=MESH)

    @pl.loop(0, groups)
    def _(g):
        for copy in kv_copies(g):
            copy.start()

    pl.semaphore_wait(barrier, heads + ctxs - 2)

    @pl.loop(0, groups)
    def _(g):
        for d in (2, 1, 3):
            a2a(g, d, h, lax.rem(h + d, heads)).start()
        qbuf[g, c, pl.ds(pl.multiple_of(h * rows, rows), rows), :] = q_ref[
            :, pl.ds(pl.multiple_of(h * hg + g * cw, cw), cw)]

    @pl.loop(0, ncols)
    def _(n):
        w_copy(n).start()

    for i in range(kept_ref.shape[0]):
        bias[:, i * 128:(i + 1) * 128] = jnp.full(
            (8, 128), jnp.where(kept_ref[i] > 0, 0.0, -jnp.inf), jnp.float32)

    @pl.loop(0, groups)
    def _(g):
        for d in range(1, heads):
            a2a(g, d, lax.rem(h + heads - d, heads), h).wait_recv()
        for d in range(1, ctxs):
            gather(g, d, c, lax.rem(c + d, ctxs)).start()

    ones = jnp.ones((kbuf.shape[1], HD), jnp.bfloat16)
    lane = lax.broadcasted_iota(jnp.int32, (2 * block, HD), 1)

    @pl.loop(0, groups)
    def _(g):
        for d in range(1, ctxs):
            gather(g, d, lax.rem(c + ctxs - d, ctxs), c).wait_recv()
        for copy in kv_copies(g):
            copy.wait()
        stats = [jnp.zeros((2 * block, HD), jnp.float32) for _ in range(ctxs // 2)]
        for j in range(per):
            cols = slice(j * HD, (j + 1) * HD)
            key_head = kbuf[g, :, cols]
            value_head = jnp.concatenate([vbuf[g, :, cols], ones], axis=1)
            for t in range(ctxs // 2):
                query = qbuf[g, 2 * t:2 * t + 2, :, cols].reshape(2 * block, HD)
                scores = lax.dot_general(
                    query, key_head, (((1,), (1,)), ((), ())),
                    preferred_element_type=jnp.float32) + bias[0:1, :]
                highest = jnp.max(scores, axis=1, keepdims=True)
                probs = jnp.exp2((scores - highest) * SCALE2)
                mixed = jnp.dot(
                    probs.astype(jnp.bfloat16), value_head, preferred_element_type=jnp.float32)
                normal = mixed[:, HD:]
                abuf[g, 2 * t:2 * t + 2, :, cols] = (
                    (mixed[:, :HD] / normal).astype(jnp.bfloat16).reshape(2, block, HD))
                stats[t] = jnp.where(lane == j, highest * SCALE2 + jnp.log2(normal), stats[t])
        for t in range(ctxs // 2):
            for u in range(2):
                sbuf[g, 2 * t + u] = stats[t][u * block:(u + 1) * block].T[0:8, :]
        for d in range(1, ctxs):
            for copy in scatter(g, d, lax.rem(c + d, ctxs)):
                copy.start()

    @pl.loop(0, groups)
    def _(g):
        for d in range(1, ctxs):
            for copy in scatter(g, d, lax.rem(c + d, ctxs)):
                copy.wait_recv()
        logs = jnp.concatenate(
            [sbuf[g, c]] + [srbuf[g, d] for d in range(ctxs - 1)]
            + [jnp.zeros((HD - 8 * ctxs, block), jnp.float32)], axis=0).T
        parts = [abuf[g, c]] + [rbuf[g, d] for d in range(ctxs - 1)]
        for j in range(per):
            own = [logs[:, 8 * i + j:8 * i + j + 1] for i in range(ctxs)]
            top = functools.reduce(jnp.maximum, own)
            weights = [jnp.exp2(x - top) for x in own]
            total = functools.reduce(jnp.add, weights)
            value = functools.reduce(jnp.add, [
                w * x[:, j * HD:(j + 1) * HD].astype(jnp.float32) for w, x in zip(weights, parts)])
            att[g, :, j * HD:(j + 1) * HD] = (value / total).astype(jnp.bfloat16)

    @pl.loop(0, ncols)
    def _(n):
        w_copy(n).wait()
        total = functools.reduce(jnp.add, [
            jnp.dot(att[g], wbuf[n, g * cw:(g + 1) * cw, :], preferred_element_type=jnp.float32)
            for g in range(groups)])
        pbuf[n] = total.astype(jnp.bfloat16).reshape(heads, rows, nw)
        for i in range(2):
            to_sibling(n, i).start()

    @pl.loop(0, ncols)
    def _(n):
        to_sibling(n, 0).wait_recv()
        xsend[n] = (pbuf[n, across].astype(jnp.float32) + sib[n, 0].astype(jnp.float32)).astype(jnp.bfloat16)
        to_across(n).start()

    for n in range(ncols):
        to_sibling(n, 1).wait_recv()
        to_across(n).wait_recv()
        out_ref[:, n * nw:(n + 1) * nw] = (
            pbuf[n, h].astype(jnp.float32) + sib[n, 1].astype(jnp.float32)
            + xrecv[n].astype(jnp.float32)).astype(jnp.bfloat16)

    @pl.loop(0, groups)
    def _(g):
        for d in range(1, heads):
            a2a(g, d, h, lax.rem(h + d, heads)).wait_send()
        for d in range(1, ctxs):
            gather(g, d, c, lax.rem(c + d, ctxs)).wait_send()
            for copy in scatter(g, d, lax.rem(c + d, ctxs)):
                copy.wait_send()

    @pl.loop(0, ncols)
    def _(n):
        to_sibling(n, 0).wait_send()
        to_sibling(n, 1).wait_send()
        to_across(n).wait_send()


def fused_shards(ctxs, queries, keys, values, kept_rows, out_weight):
    rows, width = queries.shape
    key_count, hg = keys.shape
    cw = 2 * HD
    groups = hg // cw
    block = 4 * rows
    nw = 1024
    ncols = width // nw
    bf, f32 = jnp.bfloat16, jnp.float32
    dma = pltpu.SemaphoreType.DMA
    vmem = pl.BlockSpec(memory_space=pltpu.VMEM)
    hbm = pl.BlockSpec(memory_space=pl.ANY)
    return pl.pallas_call(
        kernel,
        out_shape=jax.ShapeDtypeStruct((rows, width), bf),
        in_specs=[vmem, hbm, hbm, pl.BlockSpec(memory_space=pltpu.SMEM), hbm],
        out_specs=vmem,
        scratch_shapes=[
            pltpu.VMEM((groups, key_count, cw), bf),
            pltpu.VMEM((groups, key_count, cw), bf),
            pltpu.VMEM((ncols, hg, nw), bf),
            pltpu.VMEM((groups, ctxs, block, cw), bf),
            pltpu.VMEM((groups, ctxs, block, cw), bf),
            pltpu.VMEM((groups, ctxs, 8, block), f32),
            pltpu.VMEM((groups, ctxs - 1, block, cw), bf),
            pltpu.VMEM((groups, ctxs - 1, 8, block), f32),
            pltpu.VMEM((8, key_count), f32),
            pltpu.VMEM((groups, block, cw), bf),
            pltpu.VMEM((ncols, 4, rows, nw), bf),
            pltpu.VMEM((ncols, 2, rows, nw), bf),
            pltpu.VMEM((ncols, rows, nw), bf),
            pltpu.VMEM((ncols, rows, nw), bf),
            dma((2, groups)), dma((ncols,)),
            dma((groups, 3)), dma((groups, 3)),
            dma((groups, ctxs - 1)), dma((groups, ctxs - 1)),
            dma((groups, ctxs - 1)), dma((groups, ctxs - 1)),
            dma((groups, ctxs - 1)), dma((groups, ctxs - 1)),
            dma((ncols, 2)), dma((ncols, 2)),
            dma((ncols,)), dma((ncols,)),
        ],
        compiler_params=pltpu.CompilerParams(
            collective_id=0, has_side_effects=True, vmem_limit_bytes=60 * 2**20),
        cost_estimate=pl.CostEstimate(
            flops=4 * ctxs * block * key_count * hg + 2 * block * hg * width,
            bytes_accessed=2 * (2 * key_count * hg + hg * width),
            transcendentals=ctxs * block * key_count * hg // HD),
        name="attention",
    )(queries, keys, values, kept_rows, out_weight)


def solution(mesh):
    heads, ctxs = mesh.shape["head"], mesh.shape["ctx"]

    def shards(queries, keys, values, kept_rows, out_weight):
        rows = queries.shape[0]
        if heads == 4 and ctxs == 4 and rows == 32 and keys.shape[1] % (2 * HD) == 0:
            return fused_shards(ctxs, queries, keys, values, kept_rows, out_weight)
        return general_shards(queries, keys, values, kept_rows, out_weight)

    placed = (
        P(("abl", "head", "ctx"), None),
        P(("abl", "ctx"), "head"),
        P(("abl", "ctx"), "head"),
        P(("abl", "ctx")),
        P("head", None),
    )
    return jax.shard_map(
        shards,
        mesh=mesh,
        in_specs=placed,
        out_specs=P(("abl", "head", "ctx"), None),
        check_vma=False,
    )
```

```python
import functools
import math

import jax
import jax.numpy as jnp
from jax import lax
from jax.experimental import pallas as pl
from jax.experimental.pallas import tpu as pltpu
from jax.sharding import PartitionSpec as P

HD = 128
MESH = pl.DeviceIdType.MESH
SCALE2 = math.log2(math.e) / math.sqrt(HD)


def general_shards(queries, keys, values, kept_rows, out_weight):
    score_scale = 1.0 / math.sqrt(HD)
    local_heads = keys.shape[1] // HD
    key_count = keys.shape[0]
    key_heads = keys.reshape(key_count, local_heads, HD)
    value_heads = values.reshape(key_count, local_heads, HD)
    visible = jnp.repeat(kept_rows, 128) > 0
    query_block = lax.all_to_all(queries, "head", split_axis=1, concat_axis=0, tiled=True)
    all_queries = lax.all_gather(query_block, "ctx", axis=0, tiled=True)
    row_count = all_queries.shape[0]
    shaped = all_queries.reshape(row_count, local_heads, HD)
    scores = (
        jnp.einsum("qhd,khd->hqk", shaped, key_heads, preferred_element_type=jnp.float32)
        * score_scale
    )
    scores = jnp.where(visible[None, None, :], scores, -jnp.inf)
    running = jnp.max(scores, axis=-1)
    softened = jnp.exp(scores - running[..., None])
    normal_sum = jnp.sum(softened, axis=-1)
    mixed = jnp.einsum(
        "hqk,khd->qhd",
        softened.astype(jnp.bfloat16),
        value_heads,
        preferred_element_type=jnp.float32,
    )
    summed = mixed.reshape(row_count, local_heads * HD)
    highest = lax.pmax(running, "ctx")
    rescale = jnp.exp(running - highest)
    summed = summed * jnp.repeat(rescale.T, HD, axis=1)
    normal_sum = normal_sum * rescale
    summed, normal_sum = (
        lax.psum_scatter(
            summed.astype(jnp.bfloat16), "ctx", scatter_dimension=0, tiled=True
        ).astype(jnp.float32),
        lax.psum_scatter(
            normal_sum.astype(jnp.bfloat16), "ctx", scatter_dimension=1, tiled=True
        ).astype(jnp.float32),
    )
    attended = (summed / jnp.repeat(normal_sum.T, HD, axis=1)).astype(jnp.bfloat16)
    return lax.psum_scatter(
        jnp.dot(attended, out_weight, preferred_element_type=jnp.float32).astype(jnp.bfloat16),
        "head",
        scatter_dimension=0,
        tiled=True,
    )


def kernel(
    q_hbm, k_hbm, v_hbm, kept_ref, w_hbm, out_ref,
    kbuf, vbuf, wbuf, qbuf, abuf, sbuf, rbuf, srbuf, bias, att, pbuf, sib, xsend, xrecv,
    kv_sem, w_sem, own_sem, up_s, up_r, dn_s, dn_r, a2a_s, a2a_r, ag_s, ag_r, rs_s, rs_r, st_s, st_r, sib_s, sib_r, x_s, x_r,
):
    heads, ctxs = 4, qbuf.shape[1]
    groups, _, block, cw = qbuf.shape
    rows = q_hbm.shape[0]
    hg = groups * cw
    per = cw // HD
    ncols, _, _, nw = pbuf.shape
    h = lax.axis_index("head")
    c = lax.axis_index("ctx")

    def kv_copies(g):
        cols = pl.ds(pl.multiple_of(g * cw, cw), cw)
        return (
            pltpu.make_async_copy(k_hbm.at[:, cols], kbuf.at[g], kv_sem.at[0, g]),
            pltpu.make_async_copy(v_hbm.at[:, cols], vbuf.at[g], kv_sem.at[1, g]),
        )

    def w_copy(n):
        cols = pl.ds(pl.multiple_of(n * nw, nw), nw)
        return pltpu.make_async_copy(w_hbm.at[:, cols], wbuf.at[n], w_sem.at[n])

    def a2a(g, d, sender, target):
        return pltpu.make_async_remote_copy(
            src_ref=q_hbm.at[:, pl.ds(pl.multiple_of(target * hg + g * cw, cw), cw)],
            dst_ref=qbuf.at[g, c, pl.ds(pl.multiple_of(sender * rows, rows), rows), :],
            send_sem=a2a_s.at[g, d - 1], recv_sem=a2a_r.at[g, d - 1],
            device_id={"head": target}, device_id_type=MESH)

    def own_copy(g):
        return pltpu.make_async_copy(
            q_hbm.at[:, pl.ds(pl.multiple_of(h * hg + g * cw, cw), cw)],
            qbuf.at[g, c, pl.ds(pl.multiple_of(h * rows, rows), rows), :], own_sem.at[g])

    def gather(d, sender, target):
        return pltpu.make_async_remote_copy(
            src_ref=qbuf.at[0, sender], dst_ref=qbuf.at[0, sender],
            send_sem=ag_s.at[d - 1], recv_sem=ag_r.at[d - 1],
            device_id={"ctx": target}, device_id_type=MESH)

    def up(g, k, part):
        return pltpu.make_async_remote_copy(
            src_ref=qbuf.at[g, part], dst_ref=qbuf.at[g, part],
            send_sem=up_s.at[g, k], recv_sem=up_r.at[g, k],
            device_id={"ctx": lax.rem(c + 1, ctxs)}, device_id_type=MESH)

    def down(g, k, part):
        return pltpu.make_async_remote_copy(
            src_ref=qbuf.at[g, part], dst_ref=qbuf.at[g, part],
            send_sem=dn_s.at[g, k], recv_sem=dn_r.at[g, k],
            device_id={"ctx": lax.rem(c + ctxs - 1, ctxs)}, device_id_type=MESH)

    last = ctxs - 1

    def exchanged(g):
        own_copy(g).wait()
        for d in range(1, heads):
            a2a(g, d, lax.rem(h + heads - d, heads), h).wait_recv()

    def hop(g, k):
        @pl.when(jnp.logical_and(c < last, c >= k))
        def _():
            if k:
                up(g, k - 1, c - k).wait_recv()
            up(g, k, c - k).start()

        @pl.when(jnp.logical_and(c > 0, c + k <= last))
        def _():
            if k:
                down(g, k - 1, c + k).wait_recv()
            down(g, k, c + k).start()

    def stage(s):
        for k in range(last):
            g = s - k
            inside = jnp.logical_and(g >= 1, g < groups)

            @pl.when(inside)
            def _():
                if k == 0:
                    exchanged(g)
                hop(g, k)

    def scatter(g, d, target):
        return (
            pltpu.make_async_remote_copy(
                src_ref=abuf.at[g, target], dst_ref=rbuf.at[g, d - 1],
                send_sem=rs_s.at[g, d - 1], recv_sem=rs_r.at[g, d - 1],
                device_id={"ctx": target}, device_id_type=MESH),
            pltpu.make_async_remote_copy(
                src_ref=sbuf.at[g, target], dst_ref=srbuf.at[g, d - 1],
                send_sem=st_s.at[g, d - 1], recv_sem=st_r.at[g, d - 1],
                device_id={"ctx": target}, device_id_type=MESH),
        )

    sibling = h + 1 - 2 * lax.rem(h, 2)
    across = lax.rem(h + 2, 4)
    diagonal = lax.rem(sibling + 2, 4)

    def to_sibling(n, i):
        return pltpu.make_async_remote_copy(
            src_ref=pbuf.at[n, sibling if i else diagonal], dst_ref=sib.at[n, i],
            send_sem=sib_s.at[n, i], recv_sem=sib_r.at[n, i],
            device_id={"head": sibling}, device_id_type=MESH)

    def to_across(n):
        return pltpu.make_async_remote_copy(
            src_ref=xsend.at[n], dst_ref=xrecv.at[n],
            send_sem=x_s.at[n], recv_sem=x_r.at[n],
            device_id={"head": across}, device_id_type=MESH)

    def send_across(n):
        to_sibling(n, 0).wait_recv()
        xsend[n] = (pbuf[n, across].astype(jnp.float32) + sib[n, 0].astype(jnp.float32)).astype(jnp.bfloat16)
        to_across(n).start()

    barrier = pltpu.get_barrier_semaphore()
    for d in range(1, heads):
        pl.semaphore_signal(barrier, inc=1, device_id={"head": lax.rem(h + d, heads)}, device_id_type=MESH)
    for d in range(1, ctxs):
        pl.semaphore_signal(barrier, inc=1, device_id={"ctx": lax.rem(c + d, ctxs)}, device_id_type=MESH)

    @pl.loop(0, groups)
    def _(g):
        for copy in kv_copies(g):
            copy.start()

    pl.semaphore_wait(barrier, heads + ctxs - 2)

    @pl.loop(0, groups)
    def _(g):
        for d in (2, 1, 3):
            a2a(g, d, h, lax.rem(h + d, heads)).start()
        own_copy(g).start()

    @pl.loop(0, ncols)
    def _(n):
        w_copy(n).start()

    for i in range(kept_ref.shape[0]):
        bias[:, i * 128:(i + 1) * 128] = jnp.full(
            (8, 128), jnp.where(kept_ref[i] > 0, 0.0, -jnp.inf), jnp.float32)

    exchanged(0)
    for d in (2, 1, 3):
        gather(d, c, lax.rem(c + d, ctxs)).start()
    stage(1)
    stage(2)

    ones = jnp.ones((kbuf.shape[1], HD), jnp.bfloat16)
    lane = lax.broadcasted_iota(jnp.int32, (2 * block, HD), 1)

    @pl.loop(0, groups)
    def _(g):
        @pl.when(g == 0)
        def _():
            for d in range(1, ctxs):
                gather(d, lax.rem(c + ctxs - d, ctxs), c).wait_recv()

        @pl.when(jnp.logical_and(g > 0, c == last))
        def _():
            for k in range(last):
                up(g, k, last - 1 - k).wait_recv()

        @pl.when(jnp.logical_and(g > 0, c == 0))
        def _():
            for k in range(last):
                down(g, k, 1 + k).wait_recv()

        for copy in kv_copies(g):
            copy.wait()
        stats = [jnp.zeros((2 * block, HD), jnp.float32) for _ in range(ctxs // 2)]
        for j in range(per):
            if j == 1:
                stage(g + 3)
            cols = slice(j * HD, (j + 1) * HD)
            key_head = kbuf[g, :, cols]
            value_head = jnp.concatenate([vbuf[g, :, cols], ones], axis=1)
            for t in range(ctxs // 2):
                query = qbuf[g, 2 * t:2 * t + 2, :, cols].reshape(2 * block, HD)
                scores = lax.dot_general(
                    query, key_head, (((1,), (1,)), ((), ())),
                    preferred_element_type=jnp.float32) + bias[0:1, :]
                highest = jnp.max(scores, axis=1, keepdims=True)
                probs = jnp.exp2((scores - highest) * SCALE2)
                mixed = jnp.dot(
                    probs.astype(jnp.bfloat16), value_head, preferred_element_type=jnp.float32)
                normal = mixed[:, HD:]
                abuf[g, 2 * t:2 * t + 2, :, cols] = (
                    (mixed[:, :HD] / normal).astype(jnp.bfloat16).reshape(2, block, HD))
                stats[t] = jnp.where(lane == j, highest * SCALE2 + jnp.log2(normal), stats[t])
        for t in range(ctxs // 2):
            for u in range(2):
                sbuf[g, 2 * t + u] = stats[t][u * block:(u + 1) * block].T[0:8, :]
        for d in range(1, ctxs):
            for copy in scatter(g, d, lax.rem(c + d, ctxs)):
                copy.start()

    @pl.loop(0, groups)
    def _(g):
        for d in range(1, ctxs):
            for copy in scatter(g, d, lax.rem(c + d, ctxs)):
                copy.wait_recv()
        logs = jnp.concatenate(
            [sbuf[g, c]] + [srbuf[g, d] for d in range(ctxs - 1)]
            + [jnp.zeros((HD - 8 * ctxs, block), jnp.float32)], axis=0).T
        parts = [abuf[g, c]] + [rbuf[g, d] for d in range(ctxs - 1)]
        for j in range(per):
            own = [logs[:, 8 * i + j:8 * i + j + 1] for i in range(ctxs)]
            top = functools.reduce(jnp.maximum, own)
            weights = [jnp.exp2(x - top) for x in own]
            total = functools.reduce(jnp.add, weights)
            value = functools.reduce(jnp.add, [
                w * x[:, j * HD:(j + 1) * HD].astype(jnp.float32) for w, x in zip(weights, parts)])
            att[g, :, j * HD:(j + 1) * HD] = (value / total).astype(jnp.bfloat16)

    @pl.loop(0, ncols)
    def _(n):
        w_copy(n).wait()
        total = functools.reduce(jnp.add, [
            jnp.dot(att[g], wbuf[n, g * cw:(g + 1) * cw, :], preferred_element_type=jnp.float32)
            for g in range(groups)])
        pbuf[n] = total.astype(jnp.bfloat16).reshape(heads, rows, nw)
        for i in range(2):
            to_sibling(n, i).start()

        @pl.when(n > 0)
        def _():
            send_across(n - 1)

    send_across(ncols - 1)

    for n in range(ncols):
        to_sibling(n, 1).wait_recv()
        to_across(n).wait_recv()
        out_ref[:, n * nw:(n + 1) * nw] = (
            pbuf[n, h].astype(jnp.float32) + sib[n, 1].astype(jnp.float32)
            + xrecv[n].astype(jnp.float32)).astype(jnp.bfloat16)

    @pl.loop(0, groups)
    def _(g):
        for d in range(1, heads):
            a2a(g, d, h, lax.rem(h + d, heads)).wait_send()
        for k in range(last):
            @pl.when(jnp.logical_and(g > 0, jnp.logical_and(c < last, c >= k)))
            def _():
                up(g, k, c - k).wait_send()

            @pl.when(jnp.logical_and(g > 0, jnp.logical_and(c > 0, c + k <= last)))
            def _():
                down(g, k, c + k).wait_send()

        for d in range(1, ctxs):
            for copy in scatter(g, d, lax.rem(c + d, ctxs)):
                copy.wait_send()

    for d in range(1, ctxs):
        gather(d, c, lax.rem(c + d, ctxs)).wait_send()

    @pl.loop(0, ncols)
    def _(n):
        to_sibling(n, 0).wait_send()
        to_sibling(n, 1).wait_send()
        to_across(n).wait_send()


def fused_shards(ctxs, queries, keys, values, kept_rows, out_weight):
    rows, width = queries.shape
    key_count, hg = keys.shape
    cw = 2 * HD
    groups = hg // cw
    block = 4 * rows
    nw = 1024
    ncols = width // nw
    bf, f32 = jnp.bfloat16, jnp.float32
    dma = pltpu.SemaphoreType.DMA
    vmem = pl.BlockSpec(memory_space=pltpu.VMEM)
    hbm = pl.BlockSpec(memory_space=pl.ANY)
    return pl.pallas_call(
        kernel,
        out_shape=jax.ShapeDtypeStruct((rows, width), bf),
        in_specs=[hbm, hbm, hbm, pl.BlockSpec(memory_space=pltpu.SMEM), hbm],
        out_specs=vmem,
        scratch_shapes=[
            pltpu.VMEM((groups, key_count, cw), bf),
            pltpu.VMEM((groups, key_count, cw), bf),
            pltpu.VMEM((ncols, hg, nw), bf),
            pltpu.VMEM((groups, ctxs, block, cw), bf),
            pltpu.VMEM((groups, ctxs, block, cw), bf),
            pltpu.VMEM((groups, ctxs, 8, block), f32),
            pltpu.VMEM((groups, ctxs - 1, block, cw), bf),
            pltpu.VMEM((groups, ctxs - 1, 8, block), f32),
            pltpu.VMEM((8, key_count), f32),
            pltpu.VMEM((groups, block, cw), bf),
            pltpu.VMEM((ncols, 4, rows, nw), bf),
            pltpu.VMEM((ncols, 2, rows, nw), bf),
            pltpu.VMEM((ncols, rows, nw), bf),
            pltpu.VMEM((ncols, rows, nw), bf),
            dma((2, groups)), dma((ncols,)), dma((groups,)),
            dma((groups, ctxs - 1)), dma((groups, ctxs - 1)),
            dma((groups, ctxs - 1)), dma((groups, ctxs - 1)),
            dma((groups, 3)), dma((groups, 3)),
            dma((ctxs - 1,)), dma((ctxs - 1,)),
            dma((groups, ctxs - 1)), dma((groups, ctxs - 1)),
            dma((groups, ctxs - 1)), dma((groups, ctxs - 1)),
            dma((ncols, 2)), dma((ncols, 2)),
            dma((ncols,)), dma((ncols,)),
        ],
        compiler_params=pltpu.CompilerParams(
            collective_id=0, has_side_effects=True, vmem_limit_bytes=60 * 2**20),
        cost_estimate=pl.CostEstimate(
            flops=4 * ctxs * block * key_count * hg + 2 * block * hg * width,
            bytes_accessed=2 * (2 * key_count * hg + hg * width),
            transcendentals=ctxs * block * key_count * hg // HD),
        name="attention",
    )(queries, keys, values, kept_rows, out_weight)


def solution(mesh):
    heads, ctxs = mesh.shape["head"], mesh.shape["ctx"]

    def shards(queries, keys, values, kept_rows, out_weight):
        rows = queries.shape[0]
        if heads == 4 and ctxs == 4 and rows == 32 and keys.shape[1] % (2 * HD) == 0:
            return fused_shards(ctxs, queries, keys, values, kept_rows, out_weight)
        return general_shards(queries, keys, values, kept_rows, out_weight)

    placed = (
        P(("abl", "head", "ctx"), None),
        P(("abl", "ctx"), "head"),
        P(("abl", "ctx"), "head"),
        P(("abl", "ctx")),
        P("head", None),
    )
    return jax.shard_map(
        shards,
        mesh=mesh,
        in_specs=placed,
        out_specs=P(("abl", "head", "ctx"), None),
        check_vma=False,
    )
```

```python
import functools
import math

import jax
import jax.numpy as jnp
from jax import lax
from jax.experimental import pallas as pl
from jax.experimental.pallas import tpu as pltpu
from jax.sharding import PartitionSpec as P

HD = 128
MESH = pl.DeviceIdType.MESH
SCALE2 = math.log2(math.e) / math.sqrt(HD)


def general_shards(queries, keys, values, kept_rows, out_weight):
    score_scale = 1.0 / math.sqrt(HD)
    local_heads = keys.shape[1] // HD
    key_count = keys.shape[0]
    key_heads = keys.reshape(key_count, local_heads, HD)
    value_heads = values.reshape(key_count, local_heads, HD)
    visible = jnp.repeat(kept_rows, 128) > 0
    query_block = lax.all_to_all(queries, "head", split_axis=1, concat_axis=0, tiled=True)
    all_queries = lax.all_gather(query_block, "ctx", axis=0, tiled=True)
    row_count = all_queries.shape[0]
    shaped = all_queries.reshape(row_count, local_heads, HD)
    scores = (
        jnp.einsum("qhd,khd->hqk", shaped, key_heads, preferred_element_type=jnp.float32)
        * score_scale
    )
    scores = jnp.where(visible[None, None, :], scores, -jnp.inf)
    running = jnp.max(scores, axis=-1)
    softened = jnp.exp(scores - running[..., None])
    normal_sum = jnp.sum(softened, axis=-1)
    mixed = jnp.einsum(
        "hqk,khd->qhd",
        softened.astype(jnp.bfloat16),
        value_heads,
        preferred_element_type=jnp.float32,
    )
    summed = mixed.reshape(row_count, local_heads * HD)
    highest = lax.pmax(running, "ctx")
    rescale = jnp.exp(running - highest)
    summed = summed * jnp.repeat(rescale.T, HD, axis=1)
    normal_sum = normal_sum * rescale
    summed, normal_sum = (
        lax.psum_scatter(
            summed.astype(jnp.bfloat16), "ctx", scatter_dimension=0, tiled=True
        ).astype(jnp.float32),
        lax.psum_scatter(
            normal_sum.astype(jnp.bfloat16), "ctx", scatter_dimension=1, tiled=True
        ).astype(jnp.float32),
    )
    attended = (summed / jnp.repeat(normal_sum.T, HD, axis=1)).astype(jnp.bfloat16)
    return lax.psum_scatter(
        jnp.dot(attended, out_weight, preferred_element_type=jnp.float32).astype(jnp.bfloat16),
        "head",
        scatter_dimension=0,
        tiled=True,
    )


def kernel(
    q_hbm, k_hbm, v_hbm, kept_ref, w_hbm, out_ref,
    kbuf, vbuf, wbuf, qbuf, abuf, sbuf, rbuf, srbuf, dbuf, dlog, ubuf, ulog, bias, att, pbuf, sib, xsend, xrecv,
    kv_sem, w_sem, own_sem, up_s, up_r, dn_s, dn_r, a2a_s, a2a_r, ag_s, ag_r, rs_s, rs_r, st_s, st_r,
    pd_s, pd_r, pu_s, pu_r, sib_s, sib_r, x_s, x_r,
):
    heads, ctxs = 4, qbuf.shape[1]
    groups, _, block, cw = qbuf.shape
    rows = q_hbm.shape[0]
    hg = groups * cw
    per = cw // HD
    ncols, _, _, nw = pbuf.shape
    last = ctxs - 1
    h = lax.axis_index("head")
    c = lax.axis_index("ctx")

    def kv_copies(g):
        cols = pl.ds(pl.multiple_of(g * cw, cw), cw)
        return (
            pltpu.make_async_copy(k_hbm.at[:, cols], kbuf.at[g], kv_sem.at[0, g]),
            pltpu.make_async_copy(v_hbm.at[:, cols], vbuf.at[g], kv_sem.at[1, g]),
        )

    def w_copy(n):
        cols = pl.ds(pl.multiple_of(n * nw, nw), nw)
        return pltpu.make_async_copy(w_hbm.at[:, cols], wbuf.at[n], w_sem.at[n])

    def a2a(g, d, sender, target):
        return pltpu.make_async_remote_copy(
            src_ref=q_hbm.at[:, pl.ds(pl.multiple_of(target * hg + g * cw, cw), cw)],
            dst_ref=qbuf.at[g, c, pl.ds(pl.multiple_of(sender * rows, rows), rows), :],
            send_sem=a2a_s.at[g, d - 1], recv_sem=a2a_r.at[g, d - 1],
            device_id={"head": target}, device_id_type=MESH)

    def own_copy(g):
        return pltpu.make_async_copy(
            q_hbm.at[:, pl.ds(pl.multiple_of(h * hg + g * cw, cw), cw)],
            qbuf.at[g, c, pl.ds(pl.multiple_of(h * rows, rows), rows), :], own_sem.at[g])

    def gather(d, sender, target):
        return pltpu.make_async_remote_copy(
            src_ref=qbuf.at[0, sender], dst_ref=qbuf.at[0, sender],
            send_sem=ag_s.at[d - 1], recv_sem=ag_r.at[d - 1],
            device_id={"ctx": target}, device_id_type=MESH)

    def up(g, k, part):
        return pltpu.make_async_remote_copy(
            src_ref=qbuf.at[g, part], dst_ref=qbuf.at[g, part],
            send_sem=up_s.at[g, k], recv_sem=up_r.at[g, k],
            device_id={"ctx": lax.rem(c + 1, ctxs)}, device_id_type=MESH)

    def down(g, k, part):
        return pltpu.make_async_remote_copy(
            src_ref=qbuf.at[g, part], dst_ref=qbuf.at[g, part],
            send_sem=dn_s.at[g, k], recv_sem=dn_r.at[g, k],
            device_id={"ctx": lax.rem(c + ctxs - 1, ctxs)}, device_id_type=MESH)

    def exchanged(g):
        own_copy(g).wait()
        for d in range(1, heads):
            a2a(g, d, lax.rem(h + heads - d, heads), h).wait_recv()

    def hop(g, k):
        @pl.when(jnp.logical_and(c < last, c >= k))
        def _():
            if k:
                up(g, k - 1, c - k).wait_recv()
            up(g, k, c - k).start()

        @pl.when(jnp.logical_and(c > 0, c + k <= last))
        def _():
            if k:
                down(g, k - 1, c + k).wait_recv()
            down(g, k, c + k).start()

    def stage(s):
        for k in range(last):
            g = s - k
            inside = jnp.logical_and(g >= 1, g < groups)

            @pl.when(inside)
            def _():
                if k == 0:
                    exchanged(g)
                hop(g, k)

    def scatter(d, target):
        return (
            pltpu.make_async_remote_copy(
                src_ref=abuf.at[groups - 1, target], dst_ref=rbuf.at[d - 1],
                send_sem=rs_s.at[d - 1], recv_sem=rs_r.at[d - 1],
                device_id={"ctx": target}, device_id_type=MESH),
            pltpu.make_async_remote_copy(
                src_ref=sbuf.at[groups - 1, target], dst_ref=srbuf.at[d - 1],
                send_sem=st_s.at[d - 1], recv_sem=st_r.at[d - 1],
                device_id={"ctx": target}, device_id_type=MESH),
        )

    def part_down(g, b):
        target = lax.rem(c + ctxs - 1, ctxs)
        return (
            pltpu.make_async_remote_copy(
                src_ref=sbuf.at[g, b], dst_ref=dlog.at[g, b],
                send_sem=pd_s.at[1, g, b], recv_sem=pd_r.at[1, g, b],
                device_id={"ctx": target}, device_id_type=MESH),
            pltpu.make_async_remote_copy(
                src_ref=abuf.at[g, b], dst_ref=dbuf.at[g, b],
                send_sem=pd_s.at[0, g, b], recv_sem=pd_r.at[0, g, b],
                device_id={"ctx": target}, device_id_type=MESH),
        )

    def part_up(g, b):
        target = lax.rem(c + 1, ctxs)
        return (
            pltpu.make_async_remote_copy(
                src_ref=sbuf.at[g, b], dst_ref=ulog.at[g, b],
                send_sem=pu_s.at[1, g, b], recv_sem=pu_r.at[1, g, b],
                device_id={"ctx": target}, device_id_type=MESH),
            pltpu.make_async_remote_copy(
                src_ref=abuf.at[g, b], dst_ref=ubuf.at[g, b],
                send_sem=pu_s.at[0, g, b], recv_sem=pu_r.at[0, g, b],
                device_id={"ctx": target}, device_id_type=MESH),
        )

    def merge(g, b, part, log):
        mine, other = sbuf[g, b], log[g, b]
        top = jnp.maximum(mine, other)
        weights = jnp.exp2(mine - top), jnp.exp2(other - top)
        total = weights[0] + weights[1]
        sbuf[g, b] = top + jnp.log2(total)
        columns = jnp.concatenate(
            [weights[0] / total, weights[1] / total, jnp.zeros((HD - 16, block), jnp.float32)], axis=0).T
        for j in range(per):
            cols = slice(j * HD, (j + 1) * HD)
            abuf[g, b, :, cols] = (
                columns[:, j:j + 1] * abuf[g, b, :, cols].astype(jnp.float32)
                + columns[:, 8 + j:9 + j] * part[g, b, :, cols].astype(jnp.float32)
            ).astype(jnp.bfloat16)

    def part_stage(g, s):
        @pl.when(c == last - s)
        def _():
            for b in range(last - s):
                if s:
                    for copy in part_down(g, b):
                        copy.wait_recv()
                    merge(g, b, dbuf, dlog)
                for copy in part_down(g, b):
                    copy.start()

        @pl.when(c == s)
        def _():
            for b in range(last, s, -1):
                if s:
                    for copy in part_up(g, b):
                        copy.wait_recv()
                    merge(g, b, ubuf, ulog)
                for copy in part_up(g, b):
                    copy.start()

    def part_final(g):
        @pl.when(c < last)
        def _():
            for copy in part_down(g, c):
                copy.wait_recv()
            merge(g, c, dbuf, dlog)

        @pl.when(c > 0)
        def _():
            for copy in part_up(g, c):
                copy.wait_recv()
            merge(g, c, ubuf, ulog)

        att[g] = abuf[g, c]

    sibling = h + 1 - 2 * lax.rem(h, 2)
    across = lax.rem(h + 2, 4)
    diagonal = lax.rem(sibling + 2, 4)

    def to_sibling(n, i):
        return pltpu.make_async_remote_copy(
            src_ref=pbuf.at[n, sibling if i else diagonal], dst_ref=sib.at[n, i],
            send_sem=sib_s.at[n, i], recv_sem=sib_r.at[n, i],
            device_id={"head": sibling}, device_id_type=MESH)

    def to_across(n):
        return pltpu.make_async_remote_copy(
            src_ref=xsend.at[n], dst_ref=xrecv.at[n],
            send_sem=x_s.at[n], recv_sem=x_r.at[n],
            device_id={"head": across}, device_id_type=MESH)

    def send_across(n):
        to_sibling(n, 0).wait_recv()
        xsend[n] = (pbuf[n, across].astype(jnp.float32) + sib[n, 0].astype(jnp.float32)).astype(jnp.bfloat16)
        to_across(n).start()

    barrier = pltpu.get_barrier_semaphore()
    for d in range(1, heads):
        pl.semaphore_signal(barrier, inc=1, device_id={"head": lax.rem(h + d, heads)}, device_id_type=MESH)
    for d in range(1, ctxs):
        pl.semaphore_signal(barrier, inc=1, device_id={"ctx": lax.rem(c + d, ctxs)}, device_id_type=MESH)

    @pl.loop(0, groups)
    def _(g):
        for copy in kv_copies(g):
            copy.start()

    pl.semaphore_wait(barrier, heads + ctxs - 2)

    @pl.loop(0, groups)
    def _(g):
        for d in (2, 1, 3):
            a2a(g, d, h, lax.rem(h + d, heads)).start()
        own_copy(g).start()

    @pl.loop(0, ncols)
    def _(n):
        w_copy(n).start()

    for i in range(kept_ref.shape[0]):
        bias[:, i * 128:(i + 1) * 128] = jnp.full(
            (8, 128), jnp.where(kept_ref[i] > 0, 0.0, -jnp.inf), jnp.float32)

    exchanged(0)
    for d in (2, 1, 3):
        gather(d, c, lax.rem(c + d, ctxs)).start()
    stage(1)
    stage(2)

    ones = jnp.ones((kbuf.shape[1], HD), jnp.bfloat16)
    lane = lax.broadcasted_iota(jnp.int32, (2 * block, HD), 1)

    @pl.loop(0, groups)
    def _(g):
        @pl.when(g == 0)
        def _():
            for d in range(1, ctxs):
                gather(d, lax.rem(c + ctxs - d, ctxs), c).wait_recv()

        @pl.when(jnp.logical_and(g > 0, c == last))
        def _():
            for k in range(last):
                up(g, k, last - 1 - k).wait_recv()

        @pl.when(jnp.logical_and(g > 0, c == 0))
        def _():
            for k in range(last):
                down(g, k, 1 + k).wait_recv()

        for copy in kv_copies(g):
            copy.wait()
        stats = [jnp.zeros((2 * block, HD), jnp.float32) for _ in range(ctxs // 2)]
        for j in range(per):
            if j == 1:
                stage(g + 3)
            cols = slice(j * HD, (j + 1) * HD)
            key_head = kbuf[g, :, cols]
            value_head = jnp.concatenate([vbuf[g, :, cols], ones], axis=1)
            for t in range(ctxs // 2):
                query = qbuf[g, 2 * t:2 * t + 2, :, cols].reshape(2 * block, HD)
                scores = lax.dot_general(
                    query, key_head, (((1,), (1,)), ((), ())),
                    preferred_element_type=jnp.float32) + bias[0:1, :]
                highest = jnp.max(scores, axis=1, keepdims=True)
                probs = jnp.exp2((scores - highest) * SCALE2)
                mixed = jnp.dot(
                    probs.astype(jnp.bfloat16), value_head, preferred_element_type=jnp.float32)
                normal = mixed[:, HD:]
                abuf[g, 2 * t:2 * t + 2, :, cols] = (
                    (mixed[:, :HD] / normal).astype(jnp.bfloat16).reshape(2, block, HD))
                stats[t] = jnp.where(lane == j, highest * SCALE2 + jnp.log2(normal), stats[t])
        for t in range(ctxs // 2):
            for u in range(2):
                sbuf[g, 2 * t + u] = stats[t][u * block:(u + 1) * block].T[0:8, :]

        @pl.when(g < groups - 1)
        def _():
            part_stage(g, 0)

        @pl.when(g == groups - 1)
        def _():
            for d in (2, 1, 3):
                for copy in scatter(d, lax.rem(c + d, ctxs)):
                    copy.start()

        @pl.when(g >= 1)
        def _():
            part_stage(g - 1, 1)

        @pl.when(g >= 2)
        def _():
            part_stage(g - 2, 2)

        @pl.when(g >= 3)
        def _():
            part_final(g - 3)

    part_stage(groups - 2, 2)
    part_final(groups - 3)
    part_final(groups - 2)

    for d in range(1, ctxs):
        for copy in scatter(d, lax.rem(c + d, ctxs)):
            copy.wait_recv()
    final = groups - 1
    logs = jnp.concatenate(
        [sbuf[final, c]] + [srbuf[d] for d in range(ctxs - 1)]
        + [jnp.zeros((HD - 8 * ctxs, block), jnp.float32)], axis=0).T
    for j in range(per):
        cols = slice(j * HD, (j + 1) * HD)
        own = [logs[:, 8 * i + j:8 * i + j + 1] for i in range(ctxs)]
        top = functools.reduce(jnp.maximum, own)
        weights = [jnp.exp2(x - top) for x in own]
        total = functools.reduce(jnp.add, weights)
        parts = [abuf[final, c, :, cols]] + [rbuf[d, :, cols] for d in range(ctxs - 1)]
        value = functools.reduce(jnp.add, [w * x.astype(jnp.float32) for w, x in zip(weights, parts)])
        att[final, :, cols] = (value / total).astype(jnp.bfloat16)

    @pl.loop(0, ncols)
    def _(n):
        w_copy(n).wait()
        total = functools.reduce(jnp.add, [
            jnp.dot(att[g], wbuf[n, g * cw:(g + 1) * cw, :], preferred_element_type=jnp.float32)
            for g in range(groups)])
        pbuf[n] = total.astype(jnp.bfloat16).reshape(heads, rows, nw)
        for i in range(2):
            to_sibling(n, i).start()

        @pl.when(n > 0)
        def _():
            send_across(n - 1)

    send_across(ncols - 1)

    for n in range(ncols):
        to_sibling(n, 1).wait_recv()
        to_across(n).wait_recv()
        out_ref[:, n * nw:(n + 1) * nw] = (
            pbuf[n, h].astype(jnp.float32) + sib[n, 1].astype(jnp.float32)
            + xrecv[n].astype(jnp.float32)).astype(jnp.bfloat16)

    @pl.loop(0, groups)
    def _(g):
        for d in range(1, heads):
            a2a(g, d, h, lax.rem(h + d, heads)).wait_send()
        for k in range(last):
            @pl.when(jnp.logical_and(g > 0, jnp.logical_and(c < last, c >= k)))
            def _():
                up(g, k, c - k).wait_send()

            @pl.when(jnp.logical_and(g > 0, jnp.logical_and(c > 0, c + k <= last)))
            def _():
                down(g, k, c + k).wait_send()

        for b in range(ctxs):
            @pl.when(jnp.logical_and(g < groups - 1, b < c))
            def _():
                for copy in part_down(g, b):
                    copy.wait_send()

            @pl.when(jnp.logical_and(g < groups - 1, b > c))
            def _():
                for copy in part_up(g, b):
                    copy.wait_send()

    for d in range(1, ctxs):
        gather(d, c, lax.rem(c + d, ctxs)).wait_send()
        for copy in scatter(d, lax.rem(c + d, ctxs)):
            copy.wait_send()

    @pl.loop(0, ncols)
    def _(n):
        to_sibling(n, 0).wait_send()
        to_sibling(n, 1).wait_send()
        to_across(n).wait_send()


def fused_shards(ctxs, queries, keys, values, kept_rows, out_weight):
    rows, width = queries.shape
    key_count, hg = keys.shape
    cw = 2 * HD
    groups = hg // cw
    block = 4 * rows
    nw = 1024
    ncols = width // nw
    bf, f32 = jnp.bfloat16, jnp.float32
    dma = pltpu.SemaphoreType.DMA
    vmem = pl.BlockSpec(memory_space=pltpu.VMEM)
    hbm = pl.BlockSpec(memory_space=pl.ANY)
    return pl.pallas_call(
        kernel,
        out_shape=jax.ShapeDtypeStruct((rows, width), bf),
        in_specs=[hbm, hbm, hbm, pl.BlockSpec(memory_space=pltpu.SMEM), hbm],
        out_specs=vmem,
        scratch_shapes=[
            pltpu.VMEM((groups, key_count, cw), bf),
            pltpu.VMEM((groups, key_count, cw), bf),
            pltpu.VMEM((ncols, hg, nw), bf),
            pltpu.VMEM((groups, ctxs, block, cw), bf),
            pltpu.VMEM((groups, ctxs, block, cw), bf),
            pltpu.VMEM((groups, ctxs, 8, block), f32),
            pltpu.VMEM((ctxs - 1, block, cw), bf),
            pltpu.VMEM((ctxs - 1, 8, block), f32),
            pltpu.VMEM((groups, ctxs, block, cw), bf),
            pltpu.VMEM((groups, ctxs, 8, block), f32),
            pltpu.VMEM((groups, ctxs, block, cw), bf),
            pltpu.VMEM((groups, ctxs, 8, block), f32),
            pltpu.VMEM((8, key_count), f32),
            pltpu.VMEM((groups, block, cw), bf),
            pltpu.VMEM((ncols, 4, rows, nw), bf),
            pltpu.VMEM((ncols, 2, rows, nw), bf),
            pltpu.VMEM((ncols, rows, nw), bf),
            pltpu.VMEM((ncols, rows, nw), bf),
            dma((2, groups)), dma((ncols,)), dma((groups,)),
            dma((groups, ctxs - 1)), dma((groups, ctxs - 1)),
            dma((groups, ctxs - 1)), dma((groups, ctxs - 1)),
            dma((groups, 3)), dma((groups, 3)),
            dma((ctxs - 1,)), dma((ctxs - 1,)),
            dma((ctxs - 1,)), dma((ctxs - 1,)),
            dma((ctxs - 1,)), dma((ctxs - 1,)),
            dma((2, groups, ctxs)), dma((2, groups, ctxs)),
            dma((2, groups, ctxs)), dma((2, groups, ctxs)),
            dma((ncols, 2)), dma((ncols, 2)),
            dma((ncols,)), dma((ncols,)),
        ],
        compiler_params=pltpu.CompilerParams(
            collective_id=0, has_side_effects=True, vmem_limit_bytes=60 * 2**20),
        cost_estimate=pl.CostEstimate(
            flops=4 * ctxs * block * key_count * hg + 2 * block * hg * width,
            bytes_accessed=2 * (2 * key_count * hg + hg * width),
            transcendentals=ctxs * block * key_count * hg // HD),
        name="attention",
    )(queries, keys, values, kept_rows, out_weight)


def solution(mesh):
    heads, ctxs = mesh.shape["head"], mesh.shape["ctx"]

    def shards(queries, keys, values, kept_rows, out_weight):
        rows = queries.shape[0]
        if heads == 4 and ctxs == 4 and rows == 32 and keys.shape[1] % (2 * HD) == 0:
            return fused_shards(ctxs, queries, keys, values, kept_rows, out_weight)
        return general_shards(queries, keys, values, kept_rows, out_weight)

    placed = (
        P(("abl", "head", "ctx"), None),
        P(("abl", "ctx"), "head"),
        P(("abl", "ctx"), "head"),
        P(("abl", "ctx")),
        P("head", None),
    )
    return jax.shard_map(
        shards,
        mesh=mesh,
        in_specs=placed,
        out_specs=P(("abl", "head", "ctx"), None),
        check_vma=False,
    )
```

```python
import functools
import math

import jax
import jax.numpy as jnp
from jax import lax
from jax.experimental import pallas as pl
from jax.experimental.pallas import tpu as pltpu
from jax.sharding import PartitionSpec as P

HD = 128
KC = 256
MESH = pl.DeviceIdType.MESH
SCALE2 = math.log2(math.e) / math.sqrt(HD)


def general_shards(queries, keys, values, kept_rows, out_weight):
    score_scale = 1.0 / math.sqrt(HD)
    local_heads = keys.shape[1] // HD
    key_count = keys.shape[0]
    key_heads = keys.reshape(key_count, local_heads, HD)
    value_heads = values.reshape(key_count, local_heads, HD)
    visible = jnp.repeat(kept_rows, 128) > 0
    query_block = lax.all_to_all(queries, "head", split_axis=1, concat_axis=0, tiled=True)
    all_queries = lax.all_gather(query_block, "ctx", axis=0, tiled=True)
    row_count = all_queries.shape[0]
    shaped = all_queries.reshape(row_count, local_heads, HD)
    scores = (
        jnp.einsum("qhd,khd->hqk", shaped, key_heads, preferred_element_type=jnp.float32)
        * score_scale
    )
    scores = jnp.where(visible[None, None, :], scores, -jnp.inf)
    running = jnp.max(scores, axis=-1)
    softened = jnp.exp(scores - running[..., None])
    normal_sum = jnp.sum(softened, axis=-1)
    mixed = jnp.einsum(
        "hqk,khd->qhd",
        softened.astype(jnp.bfloat16),
        value_heads,
        preferred_element_type=jnp.float32,
    )
    summed = mixed.reshape(row_count, local_heads * HD)
    highest = lax.pmax(running, "ctx")
    rescale = jnp.exp(running - highest)
    summed = summed * jnp.repeat(rescale.T, HD, axis=1)
    normal_sum = normal_sum * rescale
    summed, normal_sum = (
        lax.psum_scatter(
            summed.astype(jnp.bfloat16), "ctx", scatter_dimension=0, tiled=True
        ).astype(jnp.float32),
        lax.psum_scatter(
            normal_sum.astype(jnp.bfloat16), "ctx", scatter_dimension=1, tiled=True
        ).astype(jnp.float32),
    )
    attended = (summed / jnp.repeat(normal_sum.T, HD, axis=1)).astype(jnp.bfloat16)
    return lax.psum_scatter(
        jnp.dot(attended, out_weight, preferred_element_type=jnp.float32).astype(jnp.bfloat16),
        "head",
        scatter_dimension=0,
        tiled=True,
    )


def kernel(
    q_hbm, k_hbm, v_hbm, kept_ref, w_hbm, out_ref,
    kbuf, vbuf, wbuf, qbuf, abuf, sbuf, rbuf, srbuf, dbuf, dlog, ubuf, ulog, bias, att, pbuf, sib, xsend, xrecv,
    score_ref, prob_ref, top_ref,
    kv_sem, w_sem, own_sem, up_s, up_r, dn_s, dn_r, a2a_s, a2a_r, ag_s, ag_r, rs_s, rs_r, st_s, st_r,
    pd_s, pd_r, pu_s, pu_r, sib_s, sib_r, x_s, x_r,
):
    heads, ctxs = 4, qbuf.shape[1]
    groups, _, block, cw = qbuf.shape
    rows = q_hbm.shape[0]
    hg = groups * cw
    per = cw // HD
    ncols, _, _, nw = pbuf.shape
    last = ctxs - 1
    h = lax.axis_index("head")
    c = lax.axis_index("ctx")

    def kv_copies(g):
        cols = pl.ds(pl.multiple_of(g * cw, cw), cw)
        return (
            pltpu.make_async_copy(k_hbm.at[:, cols], kbuf.at[g], kv_sem.at[0, g]),
            pltpu.make_async_copy(v_hbm.at[:, cols], vbuf.at[g], kv_sem.at[1, g]),
        )

    def w_copy(n):
        cols = pl.ds(pl.multiple_of(n * nw, nw), nw)
        return pltpu.make_async_copy(w_hbm.at[:, cols], wbuf.at[n], w_sem.at[n])

    def a2a(g, d, sender, target):
        return pltpu.make_async_remote_copy(
            src_ref=q_hbm.at[:, pl.ds(pl.multiple_of(target * hg + g * cw, cw), cw)],
            dst_ref=qbuf.at[g, c, pl.ds(pl.multiple_of(sender * rows, rows), rows), :],
            send_sem=a2a_s.at[g, d - 1], recv_sem=a2a_r.at[g, d - 1],
            device_id={"head": target}, device_id_type=MESH)

    def own_copy(g):
        return pltpu.make_async_copy(
            q_hbm.at[:, pl.ds(pl.multiple_of(h * hg + g * cw, cw), cw)],
            qbuf.at[g, c, pl.ds(pl.multiple_of(h * rows, rows), rows), :], own_sem.at[g])

    def gather(d, sender, target):
        return pltpu.make_async_remote_copy(
            src_ref=qbuf.at[0, sender], dst_ref=qbuf.at[0, sender],
            send_sem=ag_s.at[d - 1], recv_sem=ag_r.at[d - 1],
            device_id={"ctx": target}, device_id_type=MESH)

    def up(g, k, part):
        return pltpu.make_async_remote_copy(
            src_ref=qbuf.at[g, part], dst_ref=qbuf.at[g, part],
            send_sem=up_s.at[g, k], recv_sem=up_r.at[g, k],
            device_id={"ctx": lax.rem(c + 1, ctxs)}, device_id_type=MESH)

    def down(g, k, part):
        return pltpu.make_async_remote_copy(
            src_ref=qbuf.at[g, part], dst_ref=qbuf.at[g, part],
            send_sem=dn_s.at[g, k], recv_sem=dn_r.at[g, k],
            device_id={"ctx": lax.rem(c + ctxs - 1, ctxs)}, device_id_type=MESH)

    def exchanged(g):
        own_copy(g).wait()
        for d in range(1, heads):
            a2a(g, d, lax.rem(h + heads - d, heads), h).wait_recv()

    def hop(g, k):
        @pl.when(jnp.logical_and(c < last, c >= k))
        def _():
            if k:
                up(g, k - 1, c - k).wait_recv()
            up(g, k, c - k).start()

        @pl.when(jnp.logical_and(c > 0, c + k <= last))
        def _():
            if k:
                down(g, k - 1, c + k).wait_recv()
            down(g, k, c + k).start()

    def stage(s):
        for k in range(last):
            g = s - k
            inside = jnp.logical_and(g >= 1, g < groups)

            @pl.when(inside)
            def _():
                if k == 0:
                    exchanged(g)
                hop(g, k)

    def scatter(d, target):
        return (
            pltpu.make_async_remote_copy(
                src_ref=abuf.at[groups - 1, target], dst_ref=rbuf.at[d - 1],
                send_sem=rs_s.at[d - 1], recv_sem=rs_r.at[d - 1],
                device_id={"ctx": target}, device_id_type=MESH),
            pltpu.make_async_remote_copy(
                src_ref=sbuf.at[groups - 1, target], dst_ref=srbuf.at[d - 1],
                send_sem=st_s.at[d - 1], recv_sem=st_r.at[d - 1],
                device_id={"ctx": target}, device_id_type=MESH),
        )

    def part_down(g, b):
        target = lax.rem(c + ctxs - 1, ctxs)
        return (
            pltpu.make_async_remote_copy(
                src_ref=sbuf.at[g, b], dst_ref=dlog.at[g, b],
                send_sem=pd_s.at[1, g, b], recv_sem=pd_r.at[1, g, b],
                device_id={"ctx": target}, device_id_type=MESH),
            pltpu.make_async_remote_copy(
                src_ref=abuf.at[g, b], dst_ref=dbuf.at[g, b],
                send_sem=pd_s.at[0, g, b], recv_sem=pd_r.at[0, g, b],
                device_id={"ctx": target}, device_id_type=MESH),
        )

    def part_up(g, b):
        target = lax.rem(c + 1, ctxs)
        return (
            pltpu.make_async_remote_copy(
                src_ref=sbuf.at[g, b], dst_ref=ulog.at[g, b],
                send_sem=pu_s.at[1, g, b], recv_sem=pu_r.at[1, g, b],
                device_id={"ctx": target}, device_id_type=MESH),
            pltpu.make_async_remote_copy(
                src_ref=abuf.at[g, b], dst_ref=ubuf.at[g, b],
                send_sem=pu_s.at[0, g, b], recv_sem=pu_r.at[0, g, b],
                device_id={"ctx": target}, device_id_type=MESH),
        )

    def merge(g, b, part, log):
        mine, other = sbuf[g, b], log[g, b]
        top = jnp.maximum(mine, other)
        weights = jnp.exp2(mine - top), jnp.exp2(other - top)
        total = weights[0] + weights[1]
        sbuf[g, b] = top + jnp.log2(total)
        columns = jnp.concatenate(
            [weights[0] / total, weights[1] / total, jnp.zeros((HD - 16, block), jnp.float32)], axis=0).T
        for j in range(per):
            cols = slice(j * HD, (j + 1) * HD)
            abuf[g, b, :, cols] = (
                columns[:, j:j + 1] * abuf[g, b, :, cols].astype(jnp.float32)
                + columns[:, 8 + j:9 + j] * part[g, b, :, cols].astype(jnp.float32)
            ).astype(jnp.bfloat16)

    def part_stage(g, s):
        @pl.when(c == last - s)
        def _():
            for b in range(last - s):
                if s:
                    for copy in part_down(g, b):
                        copy.wait_recv()
                    merge(g, b, dbuf, dlog)
                for copy in part_down(g, b):
                    copy.start()

        @pl.when(c == s)
        def _():
            for b in range(last, s, -1):
                if s:
                    for copy in part_up(g, b):
                        copy.wait_recv()
                    merge(g, b, ubuf, ulog)
                for copy in part_up(g, b):
                    copy.start()

    def part_final(g):
        @pl.when(c < last)
        def _():
            for copy in part_down(g, c):
                copy.wait_recv()
            merge(g, c, dbuf, dlog)

        @pl.when(c > 0)
        def _():
            for copy in part_up(g, c):
                copy.wait_recv()
            merge(g, c, ubuf, ulog)

        att[g] = abuf[g, c]

    sibling = h + 1 - 2 * lax.rem(h, 2)
    across = lax.rem(h + 2, 4)
    diagonal = lax.rem(sibling + 2, 4)

    def to_sibling(n, i):
        return pltpu.make_async_remote_copy(
            src_ref=pbuf.at[n, sibling if i else diagonal], dst_ref=sib.at[n, i],
            send_sem=sib_s.at[n, i], recv_sem=sib_r.at[n, i],
            device_id={"head": sibling}, device_id_type=MESH)

    def to_across(n):
        return pltpu.make_async_remote_copy(
            src_ref=xsend.at[n], dst_ref=xrecv.at[n],
            send_sem=x_s.at[n], recv_sem=x_r.at[n],
            device_id={"head": across}, device_id_type=MESH)

    def send_across(n):
        to_sibling(n, 0).wait_recv()
        xsend[n] = (pbuf[n, across].astype(jnp.float32) + sib[n, 0].astype(jnp.float32)).astype(jnp.bfloat16)
        to_across(n).start()

    barrier = pltpu.get_barrier_semaphore()
    for d in range(1, heads):
        pl.semaphore_signal(barrier, inc=1, device_id={"head": lax.rem(h + d, heads)}, device_id_type=MESH)
    for d in range(1, ctxs):
        pl.semaphore_signal(barrier, inc=1, device_id={"ctx": lax.rem(c + d, ctxs)}, device_id_type=MESH)

    @pl.loop(0, groups)
    def _(g):
        for copy in kv_copies(g):
            copy.start()

    pl.semaphore_wait(barrier, heads + ctxs - 2)

    @pl.loop(0, groups)
    def _(g):
        for d in (2, 1, 3):
            a2a(g, d, h, lax.rem(h + d, heads)).start()
        own_copy(g).start()

    @pl.loop(0, ncols)
    def _(n):
        w_copy(n).start()

    for i in range(kept_ref.shape[0]):
        bias[:, i * 128:(i + 1) * 128] = jnp.full(
            (8, 128), jnp.where(kept_ref[i] > 0, 0.0, -jnp.inf), jnp.float32)

    exchanged(0)
    for d in (2, 1, 3):
        gather(d, c, lax.rem(c + d, ctxs)).start()
    stage(1)
    stage(2)

    ones = jnp.ones((kbuf.shape[1] // 2, HD), jnp.bfloat16)
    lane = lax.broadcasted_iota(jnp.int32, (2 * block, HD), 1)

    @pl.loop(0, groups)
    def _(g):
        @pl.when(g == 0)
        def _():
            for d in range(1, ctxs):
                gather(d, lax.rem(c + ctxs - d, ctxs), c).wait_recv()

        @pl.when(jnp.logical_and(g > 0, c == last))
        def _():
            for k in range(last):
                up(g, k, last - 1 - k).wait_recv()

        @pl.when(jnp.logical_and(g > 0, c == 0))
        def _():
            for k in range(last):
                down(g, k, 1 + k).wait_recv()

        for copy in kv_copies(g):
            copy.wait()
        stage(g + 3)
        stats = [jnp.zeros((2 * block, HD), jnp.float32) for _ in range(ctxs // 2)]
        units = [(j, t) for j in range(per) for t in range(ctxs // 2)]
        key_count = kbuf.shape[1]
        chunks = key_count // KC
        tops = {}
        for u in range(len(units) + 1):
            mixed = None
            if u < len(units):
                j, t = units[u]
                query = qbuf[g, 2 * t:2 * t + 2, :, j * HD:(j + 1) * HD].reshape(2 * block, HD)
                running = None
            for kc in range(chunks):
                keys = slice(kc * KC, (kc + 1) * KC)
                if u < len(units):
                    scores = lax.dot_general(
                        query, kbuf[g, keys, j * HD:(j + 1) * HD], (((1,), (1,)), ((), ())),
                        preferred_element_type=jnp.float32) + bias[0:1, keys]
                    score_ref[u % 2, :, keys] = scores
                    for i in range(KC // HD):
                        piece = scores[:, i * HD:(i + 1) * HD]
                        running = piece if running is None else jnp.maximum(running, piece)
                if u > 0:
                    pj, pt = units[u - 1]
                    for i in range(KC // HD):
                        cols = slice(kc * KC + i * HD, kc * KC + (i + 1) * HD)
                        prob_ref[(u - 1) % 2, :, cols] = jnp.exp2(
                            (score_ref[(u - 1) % 2, :, cols] - top_ref[(u - 1) % 2]) * SCALE2
                        ).astype(jnp.bfloat16)
                    if (kc + 1) % (chunks // 2) == 0:
                        span = slice((kc + 1) * KC - key_count // 2, (kc + 1) * KC)
                        value = jnp.concatenate([vbuf[g, span, pj * HD:(pj + 1) * HD], ones], axis=1)
                        part = jnp.dot(
                            prob_ref[(u - 1) % 2, :, span], value, preferred_element_type=jnp.float32)
                        mixed = part if mixed is None else mixed + part
            if u > 0:
                normal = mixed[:, HD:]
                abuf[g, 2 * pt:2 * pt + 2, :, pj * HD:(pj + 1) * HD] = (
                    (mixed[:, :HD] / normal).astype(jnp.bfloat16).reshape(2, block, HD))
                stats[pt] = jnp.where(
                    lane == pj, top_ref[(u - 1) % 2] * SCALE2 + jnp.log2(normal), stats[pt])
            if u < len(units):
                top_ref[u % 2] = jnp.broadcast_to(
                    jnp.max(running, axis=1, keepdims=True), (2 * block, HD))
        for t in range(ctxs // 2):
            for u in range(2):
                sbuf[g, 2 * t + u] = stats[t][u * block:(u + 1) * block].T[0:8, :]

        @pl.when(g < groups - 1)
        def _():
            part_stage(g, 0)

        @pl.when(g == groups - 1)
        def _():
            for d in (2, 1, 3):
                for copy in scatter(d, lax.rem(c + d, ctxs)):
                    copy.start()

        @pl.when(g >= 1)
        def _():
            part_stage(g - 1, 1)

        @pl.when(g >= 2)
        def _():
            part_stage(g - 2, 2)

        @pl.when(g >= 3)
        def _():
            part_final(g - 3)

    part_stage(groups - 2, 2)
    part_final(groups - 3)
    part_final(groups - 2)

    for d in range(1, ctxs):
        for copy in scatter(d, lax.rem(c + d, ctxs)):
            copy.wait_recv()
    final = groups - 1
    logs = jnp.concatenate(
        [sbuf[final, c]] + [srbuf[d] for d in range(ctxs - 1)]
        + [jnp.zeros((HD - 8 * ctxs, block), jnp.float32)], axis=0).T
    for j in range(per):
        cols = slice(j * HD, (j + 1) * HD)
        own = [logs[:, 8 * i + j:8 * i + j + 1] for i in range(ctxs)]
        top = functools.reduce(jnp.maximum, own)
        weights = [jnp.exp2(x - top) for x in own]
        total = functools.reduce(jnp.add, weights)
        parts = [abuf[final, c, :, cols]] + [rbuf[d, :, cols] for d in range(ctxs - 1)]
        value = functools.reduce(jnp.add, [w * x.astype(jnp.float32) for w, x in zip(weights, parts)])
        att[final, :, cols] = (value / total).astype(jnp.bfloat16)

    @pl.loop(0, ncols)
    def _(n):
        w_copy(n).wait()
        total = functools.reduce(jnp.add, [
            jnp.dot(att[g], wbuf[n, g * cw:(g + 1) * cw, :], preferred_element_type=jnp.float32)
            for g in range(groups)])
        pbuf[n] = total.astype(jnp.bfloat16).reshape(heads, rows, nw)
        for i in range(2):
            to_sibling(n, i).start()

        @pl.when(n > 0)
        def _():
            send_across(n - 1)

    send_across(ncols - 1)

    for n in range(ncols):
        to_sibling(n, 1).wait_recv()
        to_across(n).wait_recv()
        out_ref[:, n * nw:(n + 1) * nw] = (
            pbuf[n, h].astype(jnp.float32) + sib[n, 1].astype(jnp.float32)
            + xrecv[n].astype(jnp.float32)).astype(jnp.bfloat16)

    @pl.loop(0, groups)
    def _(g):
        for d in range(1, heads):
            a2a(g, d, h, lax.rem(h + d, heads)).wait_send()
        for k in range(last):
            @pl.when(jnp.logical_and(g > 0, jnp.logical_and(c < last, c >= k)))
            def _():
                up(g, k, c - k).wait_send()

            @pl.when(jnp.logical_and(g > 0, jnp.logical_and(c > 0, c + k <= last)))
            def _():
                down(g, k, c + k).wait_send()

        for b in range(ctxs):
            @pl.when(jnp.logical_and(g < groups - 1, b < c))
            def _():
                for copy in part_down(g, b):
                    copy.wait_send()

            @pl.when(jnp.logical_and(g < groups - 1, b > c))
            def _():
                for copy in part_up(g, b):
                    copy.wait_send()

    for d in range(1, ctxs):
        gather(d, c, lax.rem(c + d, ctxs)).wait_send()
        for copy in scatter(d, lax.rem(c + d, ctxs)):
            copy.wait_send()

    @pl.loop(0, ncols)
    def _(n):
        to_sibling(n, 0).wait_send()
        to_sibling(n, 1).wait_send()
        to_across(n).wait_send()


def fused_shards(ctxs, queries, keys, values, kept_rows, out_weight):
    rows, width = queries.shape
    key_count, hg = keys.shape
    cw = 2 * HD
    groups = hg // cw
    block = 4 * rows
    nw = 1024
    ncols = width // nw
    bf, f32 = jnp.bfloat16, jnp.float32
    dma = pltpu.SemaphoreType.DMA
    vmem = pl.BlockSpec(memory_space=pltpu.VMEM)
    hbm = pl.BlockSpec(memory_space=pl.ANY)
    return pl.pallas_call(
        kernel,
        out_shape=jax.ShapeDtypeStruct((rows, width), bf),
        in_specs=[hbm, hbm, hbm, pl.BlockSpec(memory_space=pltpu.SMEM), hbm],
        out_specs=vmem,
        scratch_shapes=[
            pltpu.VMEM((groups, key_count, cw), bf),
            pltpu.VMEM((groups, key_count, cw), bf),
            pltpu.VMEM((ncols, hg, nw), bf),
            pltpu.VMEM((groups, ctxs, block, cw), bf),
            pltpu.VMEM((groups, ctxs, block, cw), bf),
            pltpu.VMEM((groups, ctxs, 8, block), f32),
            pltpu.VMEM((ctxs - 1, block, cw), bf),
            pltpu.VMEM((ctxs - 1, 8, block), f32),
            pltpu.VMEM((groups, ctxs, block, cw), bf),
            pltpu.VMEM((groups, ctxs, 8, block), f32),
            pltpu.VMEM((groups, ctxs, block, cw), bf),
            pltpu.VMEM((groups, ctxs, 8, block), f32),
            pltpu.VMEM((8, key_count), f32),
            pltpu.VMEM((groups, block, cw), bf),
            pltpu.VMEM((ncols, 4, rows, nw), bf),
            pltpu.VMEM((ncols, 2, rows, nw), bf),
            pltpu.VMEM((ncols, rows, nw), bf),
            pltpu.VMEM((ncols, rows, nw), bf),
            pltpu.VMEM((2, 2 * block, key_count), f32),
            pltpu.VMEM((2, 2 * block, key_count), bf),
            pltpu.VMEM((2, 2 * block, HD), f32),
            dma((2, groups)), dma((ncols,)), dma((groups,)),
            dma((groups, ctxs - 1)), dma((groups, ctxs - 1)),
            dma((groups, ctxs - 1)), dma((groups, ctxs - 1)),
            dma((groups, 3)), dma((groups, 3)),
            dma((ctxs - 1,)), dma((ctxs - 1,)),
            dma((ctxs - 1,)), dma((ctxs - 1,)),
            dma((ctxs - 1,)), dma((ctxs - 1,)),
            dma((2, groups, ctxs)), dma((2, groups, ctxs)),
            dma((2, groups, ctxs)), dma((2, groups, ctxs)),
            dma((ncols, 2)), dma((ncols, 2)),
            dma((ncols,)), dma((ncols,)),
        ],
        compiler_params=pltpu.CompilerParams(
            collective_id=0, has_side_effects=True, vmem_limit_bytes=62 * 2**20),
        cost_estimate=pl.CostEstimate(
            flops=4 * ctxs * block * key_count * hg + 2 * block * hg * width,
            bytes_accessed=2 * (2 * key_count * hg + hg * width),
            transcendentals=ctxs * block * key_count * hg // HD),
        name="attention",
    )(queries, keys, values, kept_rows, out_weight)


def solution(mesh):
    heads, ctxs = mesh.shape["head"], mesh.shape["ctx"]

    def shards(queries, keys, values, kept_rows, out_weight):
        rows = queries.shape[0]
        if heads == 4 and ctxs == 4 and rows == 32 and keys.shape[1] % (2 * HD) == 0:
            return fused_shards(ctxs, queries, keys, values, kept_rows, out_weight)
        return general_shards(queries, keys, values, kept_rows, out_weight)

    placed = (
        P(("abl", "head", "ctx"), None),
        P(("abl", "ctx"), "head"),
        P(("abl", "ctx"), "head"),
        P(("abl", "ctx")),
        P("head", None),
    )
    return jax.shard_map(
        shards,
        mesh=mesh,
        in_specs=placed,
        out_specs=P(("abl", "head", "ctx"), None),
        check_vma=False,
    )
```

```python
import functools
import math

import jax
import jax.numpy as jnp
from jax import lax
from jax.experimental import pallas as pl
from jax.experimental.pallas import tpu as pltpu
from jax.sharding import PartitionSpec as P

HD = 128
KC = 256
MESH = pl.DeviceIdType.MESH
SCALE2 = math.log2(math.e) / math.sqrt(HD)


def general_shards(queries, keys, values, kept_rows, out_weight):
    score_scale = 1.0 / math.sqrt(HD)
    local_heads = keys.shape[1] // HD
    key_count = keys.shape[0]
    key_heads = keys.reshape(key_count, local_heads, HD)
    value_heads = values.reshape(key_count, local_heads, HD)
    visible = jnp.repeat(kept_rows, 128) > 0
    query_block = lax.all_to_all(queries, "head", split_axis=1, concat_axis=0, tiled=True)
    all_queries = lax.all_gather(query_block, "ctx", axis=0, tiled=True)
    row_count = all_queries.shape[0]
    shaped = all_queries.reshape(row_count, local_heads, HD)
    scores = (
        jnp.einsum("qhd,khd->hqk", shaped, key_heads, preferred_element_type=jnp.float32)
        * score_scale
    )
    scores = jnp.where(visible[None, None, :], scores, -jnp.inf)
    running = jnp.max(scores, axis=-1)
    softened = jnp.exp(scores - running[..., None])
    normal_sum = jnp.sum(softened, axis=-1)
    mixed = jnp.einsum(
        "hqk,khd->qhd",
        softened.astype(jnp.bfloat16),
        value_heads,
        preferred_element_type=jnp.float32,
    )
    summed = mixed.reshape(row_count, local_heads * HD)
    highest = lax.pmax(running, "ctx")
    rescale = jnp.exp(running - highest)
    summed = summed * jnp.repeat(rescale.T, HD, axis=1)
    normal_sum = normal_sum * rescale
    summed, normal_sum = (
        lax.psum_scatter(
            summed.astype(jnp.bfloat16), "ctx", scatter_dimension=0, tiled=True
        ).astype(jnp.float32),
        lax.psum_scatter(
            normal_sum.astype(jnp.bfloat16), "ctx", scatter_dimension=1, tiled=True
        ).astype(jnp.float32),
    )
    attended = (summed / jnp.repeat(normal_sum.T, HD, axis=1)).astype(jnp.bfloat16)
    return lax.psum_scatter(
        jnp.dot(attended, out_weight, preferred_element_type=jnp.float32).astype(jnp.bfloat16),
        "head",
        scatter_dimension=0,
        tiled=True,
    )


def kernel(
    q_hbm, k_hbm, v_hbm, kept_ref, w_hbm, out_ref,
    kbuf, vbuf, wbuf, qbuf, abuf, sbuf, rbuf, srbuf, dbuf, dlog, ubuf, ulog, bias, att, pbuf, sib, xsend, xrecv,
    score_ref, prob_ref, top_ref,
    kv_sem, w_sem, own_sem, up_s, up_r, dn_s, dn_r, a2a_s, a2a_r, ag_s, ag_r, rs_s, rs_r, st_s, st_r,
    pd_s, pd_r, pu_s, pu_r, sib_s, sib_r, x_s, x_r,
):
    heads, ctxs = 4, qbuf.shape[1]
    groups = kbuf.shape[0]
    slots, _, block, cw = qbuf.shape
    rows = q_hbm.shape[0] // 2
    hg = groups * cw
    per = cw // HD
    ncols, _, nw = wbuf.shape
    last = ctxs - 1
    h = lax.axis_index("head")
    c = lax.axis_index("ctx")

    def kv_copies(g):
        cols = pl.ds(pl.multiple_of(g * cw, cw), cw)
        return (
            pltpu.make_async_copy(k_hbm.at[:, cols], kbuf.at[g], kv_sem.at[0, g]),
            pltpu.make_async_copy(v_hbm.at[:, cols], vbuf.at[g], kv_sem.at[1, g]),
        )

    def w_copy(n):
        cols = pl.ds(pl.multiple_of(n * nw, nw), nw)
        return pltpu.make_async_copy(w_hbm.at[:, cols], wbuf.at[n], w_sem.at[n])

    def query_part(i, target):
        first = target * hg + lax.rem(i, groups) * cw
        return q_hbm.at[
            pl.ds(pl.multiple_of(lax.div(i, groups) * rows, rows), rows),
            pl.ds(pl.multiple_of(first, cw), cw)]

    def a2a(g, d, sender, target):
        return pltpu.make_async_remote_copy(
            src_ref=query_part(g, target),
            dst_ref=qbuf.at[g, c, pl.ds(pl.multiple_of(sender * rows, rows), rows), :],
            send_sem=a2a_s.at[g, d - 1], recv_sem=a2a_r.at[g, d - 1],
            device_id={"head": target}, device_id_type=MESH)

    def own_copy(g):
        return pltpu.make_async_copy(
            query_part(g, h),
            qbuf.at[g, c, pl.ds(pl.multiple_of(h * rows, rows), rows), :], own_sem.at[g])

    def gather(d, sender, target):
        return pltpu.make_async_remote_copy(
            src_ref=qbuf.at[0, sender], dst_ref=qbuf.at[0, sender],
            send_sem=ag_s.at[d - 1], recv_sem=ag_r.at[d - 1],
            device_id={"ctx": target}, device_id_type=MESH)

    def up(g, k, part):
        return pltpu.make_async_remote_copy(
            src_ref=qbuf.at[g, part], dst_ref=qbuf.at[g, part],
            send_sem=up_s.at[g, k], recv_sem=up_r.at[g, k],
            device_id={"ctx": lax.rem(c + 1, ctxs)}, device_id_type=MESH)

    def down(g, k, part):
        return pltpu.make_async_remote_copy(
            src_ref=qbuf.at[g, part], dst_ref=qbuf.at[g, part],
            send_sem=dn_s.at[g, k], recv_sem=dn_r.at[g, k],
            device_id={"ctx": lax.rem(c + ctxs - 1, ctxs)}, device_id_type=MESH)

    def exchanged(g):
        own_copy(g).wait()
        for d in range(1, heads):
            a2a(g, d, lax.rem(h + heads - d, heads), h).wait_recv()

    def hop(g, k):
        @pl.when(jnp.logical_and(c < last, c >= k))
        def _():
            if k:
                up(g, k - 1, c - k).wait_recv()
            up(g, k, c - k).start()

        @pl.when(jnp.logical_and(c > 0, c + k <= last))
        def _():
            if k:
                down(g, k - 1, c + k).wait_recv()
            down(g, k, c + k).start()

    def stage(s):
        for k in range(last):
            g = s - k
            inside = jnp.logical_and(g >= 1, g < slots)

            @pl.when(inside)
            def _():
                if k == 0:
                    exchanged(g)
                hop(g, k)

    def scatter(d, target):
        return (
            pltpu.make_async_remote_copy(
                src_ref=abuf.at[slots - 1, target], dst_ref=rbuf.at[d - 1],
                send_sem=rs_s.at[d - 1], recv_sem=rs_r.at[d - 1],
                device_id={"ctx": target}, device_id_type=MESH),
            pltpu.make_async_remote_copy(
                src_ref=sbuf.at[slots - 1, target], dst_ref=srbuf.at[d - 1],
                send_sem=st_s.at[d - 1], recv_sem=st_r.at[d - 1],
                device_id={"ctx": target}, device_id_type=MESH),
        )

    def part_down(g, b):
        target = lax.rem(c + ctxs - 1, ctxs)
        return (
            pltpu.make_async_remote_copy(
                src_ref=sbuf.at[g, b], dst_ref=dlog.at[g, b],
                send_sem=pd_s.at[1, g, b], recv_sem=pd_r.at[1, g, b],
                device_id={"ctx": target}, device_id_type=MESH),
            pltpu.make_async_remote_copy(
                src_ref=abuf.at[g, b], dst_ref=dbuf.at[g, b],
                send_sem=pd_s.at[0, g, b], recv_sem=pd_r.at[0, g, b],
                device_id={"ctx": target}, device_id_type=MESH),
        )

    def part_up(g, b):
        target = lax.rem(c + 1, ctxs)
        return (
            pltpu.make_async_remote_copy(
                src_ref=sbuf.at[g, b], dst_ref=ulog.at[g, b],
                send_sem=pu_s.at[1, g, b], recv_sem=pu_r.at[1, g, b],
                device_id={"ctx": target}, device_id_type=MESH),
            pltpu.make_async_remote_copy(
                src_ref=abuf.at[g, b], dst_ref=ubuf.at[g, b],
                send_sem=pu_s.at[0, g, b], recv_sem=pu_r.at[0, g, b],
                device_id={"ctx": target}, device_id_type=MESH),
        )

    def merge(g, b, part, log):
        mine, other = sbuf[g, b], log[g, b]
        top = jnp.maximum(mine, other)
        weights = jnp.exp2(mine - top), jnp.exp2(other - top)
        total = weights[0] + weights[1]
        sbuf[g, b] = top + jnp.log2(total)
        columns = jnp.concatenate(
            [weights[0] / total, weights[1] / total, jnp.zeros((HD - 16, HD), jnp.float32)], axis=0).T[0:block]
        for j in range(per):
            cols = slice(j * HD, (j + 1) * HD)
            abuf[g, b, :, cols] = (
                columns[:, j:j + 1] * abuf[g, b, :, cols].astype(jnp.float32)
                + columns[:, 8 + j:9 + j] * part[g, b, :, cols].astype(jnp.float32)
            ).astype(jnp.bfloat16)

    def part_stage(g, s):
        @pl.when(c == last - s)
        def _():
            for b in range(last - s):
                if s:
                    for copy in part_down(g, b):
                        copy.wait_recv()
                    merge(g, b, dbuf, dlog)
                for copy in part_down(g, b):
                    copy.start()

        @pl.when(c == s)
        def _():
            for b in range(last, s, -1):
                if s:
                    for copy in part_up(g, b):
                        copy.wait_recv()
                    merge(g, b, ubuf, ulog)
                for copy in part_up(g, b):
                    copy.start()

    def part_final(g):
        @pl.when(c < last)
        def _():
            for copy in part_down(g, c):
                copy.wait_recv()
            merge(g, c, dbuf, dlog)

        @pl.when(c > 0)
        def _():
            for copy in part_up(g, c):
                copy.wait_recv()
            merge(g, c, ubuf, ulog)

        att[lax.div(g, groups), :, pl.ds(pl.multiple_of(lax.rem(g, groups) * cw, cw), cw)] = abuf[g, c]

    def project(m):
        n = lax.rem(m, ncols)
        total = jnp.dot(att[lax.div(m, ncols)], wbuf[n], preferred_element_type=jnp.float32)
        pbuf[m] = total.astype(jnp.bfloat16).reshape(heads, rows, nw)
        for i in range(2):
            to_sibling(m, i).start()

    def finish(m):
        to_sibling(m, 1).wait_recv()
        to_across(m).wait_recv()
        half, n = divmod(m, ncols)
        out_ref[half * rows:(half + 1) * rows, n * nw:(n + 1) * nw] = (
            pbuf[m, h].astype(jnp.float32) + sib[m, 1].astype(jnp.float32)
            + xrecv[m].astype(jnp.float32)).astype(jnp.bfloat16)

    sibling = h + 1 - 2 * lax.rem(h, 2)
    across = lax.rem(h + 2, 4)
    diagonal = lax.rem(sibling + 2, 4)

    def to_sibling(n, i):
        return pltpu.make_async_remote_copy(
            src_ref=pbuf.at[n, sibling if i else diagonal], dst_ref=sib.at[n, i],
            send_sem=sib_s.at[n, i], recv_sem=sib_r.at[n, i],
            device_id={"head": sibling}, device_id_type=MESH)

    def to_across(n):
        return pltpu.make_async_remote_copy(
            src_ref=xsend.at[n], dst_ref=xrecv.at[n],
            send_sem=x_s.at[n], recv_sem=x_r.at[n],
            device_id={"head": across}, device_id_type=MESH)

    def send_across(n):
        to_sibling(n, 0).wait_recv()
        xsend[n] = (pbuf[n, across].astype(jnp.float32) + sib[n, 0].astype(jnp.float32)).astype(jnp.bfloat16)
        to_across(n).start()

    barrier = pltpu.get_barrier_semaphore()
    for d in range(1, heads):
        pl.semaphore_signal(barrier, inc=1, device_id={"head": lax.rem(h + d, heads)}, device_id_type=MESH)
    for d in range(1, ctxs):
        pl.semaphore_signal(barrier, inc=1, device_id={"ctx": lax.rem(c + d, ctxs)}, device_id_type=MESH)

    @pl.loop(0, groups)
    def _(g):
        for copy in kv_copies(g):
            copy.start()

    pl.semaphore_wait(barrier, heads + ctxs - 2)

    @pl.loop(0, slots)
    def _(g):
        for d in (2, 1, 3):
            a2a(g, d, h, lax.rem(h + d, heads)).start()
        own_copy(g).start()

    @pl.loop(0, ncols)
    def _(n):
        w_copy(n).start()

    for i in range(kept_ref.shape[0]):
        bias[:, i * 128:(i + 1) * 128] = jnp.full(
            (8, 128), jnp.where(kept_ref[i] > 0, 0.0, -jnp.inf), jnp.float32)

    exchanged(0)
    for d in (2, 1, 3):
        gather(d, c, lax.rem(c + d, ctxs)).start()
    stage(1)
    stage(2)

    ones = jnp.ones((kbuf.shape[1] // 2, HD), jnp.bfloat16)
    lane = lax.broadcasted_iota(jnp.int32, (ctxs * block, HD), 1)

    @pl.loop(0, slots)
    def _(g):
        group = lax.rem(g, groups)

        @pl.when(g == 0)
        def _():
            for d in range(1, ctxs):
                gather(d, lax.rem(c + ctxs - d, ctxs), c).wait_recv()

        @pl.when(jnp.logical_and(g > 0, c == last))
        def _():
            for k in range(last):
                up(g, k, last - 1 - k).wait_recv()

        @pl.when(jnp.logical_and(g > 0, c == 0))
        def _():
            for k in range(last):
                down(g, k, 1 + k).wait_recv()

        @pl.when(g < groups)
        def _():
            for copy in kv_copies(g):
                copy.wait()

        stage(g + 3)
        stats = jnp.zeros((ctxs * block, HD), jnp.float32)
        units = per
        key_count = kbuf.shape[1]
        chunks = key_count // KC
        tops = {}
        for u in range(units + 1):
            mixed = None
            if u < units:
                query = qbuf[g, :, :, u * HD:(u + 1) * HD].reshape(ctxs * block, HD)
                running = None
            for kc in range(chunks):
                keys = slice(kc * KC, (kc + 1) * KC)
                if u < units:
                    scores = lax.dot_general(
                        query, kbuf[group, keys, u * HD:(u + 1) * HD], (((1,), (1,)), ((), ())),
                        preferred_element_type=jnp.float32) + bias[0:1, keys]
                    score_ref[u % 2, :, keys] = scores
                    for i in range(KC // HD):
                        piece = scores[:, i * HD:(i + 1) * HD]
                        running = piece if running is None else jnp.maximum(running, piece)
                if u > 0:
                    pj = u - 1
                    for i in range(KC // HD):
                        cols = slice(kc * KC + i * HD, kc * KC + (i + 1) * HD)
                        prob_ref[(u - 1) % 2, :, cols] = jnp.exp2(
                            (score_ref[(u - 1) % 2, :, cols] - top_ref[(u - 1) % 2]) * SCALE2
                        ).astype(jnp.bfloat16)
                    if (kc + 1) % (chunks // 2) == 0:
                        span = slice((kc + 1) * KC - key_count // 2, (kc + 1) * KC)
                        value = jnp.concatenate([vbuf[group, span, pj * HD:(pj + 1) * HD], ones], axis=1)
                        part = jnp.dot(
                            prob_ref[(u - 1) % 2, :, span], value, preferred_element_type=jnp.float32)
                        mixed = part if mixed is None else mixed + part
            if u > 0:
                normal = mixed[:, HD:]
                abuf[g, :, :, pj * HD:(pj + 1) * HD] = (
                    (mixed[:, :HD] / normal).astype(jnp.bfloat16).reshape(ctxs, block, HD))
                stats = jnp.where(
                    lane == pj, top_ref[(u - 1) % 2] * SCALE2 + jnp.log2(normal), stats)
            if u < units:
                top_ref[u % 2] = jnp.broadcast_to(
                    jnp.max(running, axis=1, keepdims=True), (ctxs * block, HD))
        pad = jnp.zeros((HD - block, HD), jnp.float32)
        for b in range(ctxs):
            sbuf[g, b] = jnp.concatenate([stats[b * block:(b + 1) * block], pad], axis=0).T[0:8, :]

        @pl.when(g < slots - 1)
        def _():
            part_stage(g, 0)

        @pl.when(g >= 3)
        def _():
            part_final(g - 3)

        @pl.when(g >= 2)
        def _():
            part_stage(g - 2, 2)

        @pl.when(g >= 1)
        def _():
            part_stage(g - 1, 1)

        @pl.when(g == slots - 1)
        def _():
            for d in (2, 1, 3):
                for copy in scatter(d, lax.rem(c + d, ctxs)):
                    copy.start()

        begin = groups + 3
        share = ncols // (slots - begin)

        @pl.when(g == begin)
        def _():
            for n in range(ncols):
                w_copy(n).wait()

        @pl.when(g > begin)
        def _():
            for i in range(share):
                send_across((g - begin - 1) * share + i)

        @pl.when(g >= begin)
        def _():
            for i in range(share):
                project((g - begin) * share + i)

    part_stage(slots - 2, 2)
    part_final(slots - 3)
    for m in range(ncols - ncols // (groups - 3), ncols):
        send_across(m)
    part_final(slots - 2)

    for d in range(1, ctxs):
        for copy in scatter(d, lax.rem(c + d, ctxs)):
            copy.wait_recv()
    final = slots - 1
    logs = jnp.concatenate(
        [sbuf[final, c]] + [srbuf[d] for d in range(ctxs - 1)]
        + [jnp.zeros((HD - 8 * ctxs, HD), jnp.float32)], axis=0).T[0:block]
    for j in range(per):
        cols = slice(j * HD, (j + 1) * HD)
        own = [logs[:, 8 * i + j:8 * i + j + 1] for i in range(ctxs)]
        top = functools.reduce(jnp.maximum, own)
        weights = [jnp.exp2(x - top) for x in own]
        total = functools.reduce(jnp.add, weights)
        parts = [abuf[final, c, :, cols]] + [rbuf[d, :, cols] for d in range(ctxs - 1)]
        value = functools.reduce(jnp.add, [w * x.astype(jnp.float32) for w, x in zip(weights, parts)])
        first = (groups - 1) * cw + j * HD
        att[1, :, first:first + HD] = (value / total).astype(jnp.bfloat16)

    @pl.loop(0, ncols)
    def _(n):
        project(ncols + n)

        @pl.when(n > 0)
        def _():
            send_across(ncols + n - 1)

    send_across(2 * ncols - 1)

    for m in range(2 * ncols):
        finish(m)

    @pl.loop(0, slots)
    def _(g):
        for d in range(1, heads):
            a2a(g, d, h, lax.rem(h + d, heads)).wait_send()
        for k in range(last):
            @pl.when(jnp.logical_and(g > 0, jnp.logical_and(c < last, c >= k)))
            def _():
                up(g, k, c - k).wait_send()

            @pl.when(jnp.logical_and(g > 0, jnp.logical_and(c > 0, c + k <= last)))
            def _():
                down(g, k, c + k).wait_send()

        for b in range(ctxs):
            @pl.when(jnp.logical_and(g < slots - 1, b < c))
            def _():
                for copy in part_down(g, b):
                    copy.wait_send()

            @pl.when(jnp.logical_and(g < slots - 1, b > c))
            def _():
                for copy in part_up(g, b):
                    copy.wait_send()

    for d in range(1, ctxs):
        gather(d, c, lax.rem(c + d, ctxs)).wait_send()
        for copy in scatter(d, lax.rem(c + d, ctxs)):
            copy.wait_send()

    @pl.loop(0, 2 * ncols)
    def _(n):
        to_sibling(n, 0).wait_send()
        to_sibling(n, 1).wait_send()
        to_across(n).wait_send()


def fused_shards(ctxs, queries, keys, values, kept_rows, out_weight):
    rows, width = queries.shape
    key_count, hg = keys.shape
    cw = 2 * HD
    groups = hg // cw
    block = 2 * rows
    slots = 2 * groups
    nw = 1024
    ncols = width // nw
    bf, f32 = jnp.bfloat16, jnp.float32
    dma = pltpu.SemaphoreType.DMA
    vmem = pl.BlockSpec(memory_space=pltpu.VMEM)
    hbm = pl.BlockSpec(memory_space=pl.ANY)
    return pl.pallas_call(
        kernel,
        out_shape=jax.ShapeDtypeStruct((rows, width), bf),
        in_specs=[hbm, hbm, hbm, pl.BlockSpec(memory_space=pltpu.SMEM), hbm],
        out_specs=vmem,
        scratch_shapes=[
            pltpu.VMEM((groups, key_count, cw), bf),
            pltpu.VMEM((groups, key_count, cw), bf),
            pltpu.VMEM((ncols, hg, nw), bf),
            pltpu.VMEM((slots, ctxs, block, cw), bf),
            pltpu.VMEM((slots, ctxs, block, cw), bf),
            pltpu.VMEM((slots, ctxs, 8, HD), f32),
            pltpu.VMEM((ctxs - 1, block, cw), bf),
            pltpu.VMEM((ctxs - 1, 8, HD), f32),
            pltpu.VMEM((slots, ctxs, block, cw), bf),
            pltpu.VMEM((slots, ctxs, 8, HD), f32),
            pltpu.VMEM((slots, ctxs, block, cw), bf),
            pltpu.VMEM((slots, ctxs, 8, HD), f32),
            pltpu.VMEM((8, key_count), f32),
            pltpu.VMEM((2, block, hg), bf),
            pltpu.VMEM((2 * ncols, 4, rows // 2, nw), bf),
            pltpu.VMEM((2 * ncols, 2, rows // 2, nw), bf),
            pltpu.VMEM((2 * ncols, rows // 2, nw), bf),
            pltpu.VMEM((2 * ncols, rows // 2, nw), bf),
            pltpu.VMEM((2, ctxs * block, key_count), f32),
            pltpu.VMEM((2, ctxs * block, key_count), bf),
            pltpu.VMEM((2, ctxs * block, HD), f32),
            dma((2, groups)), dma((ncols,)), dma((slots,)),
            dma((slots, ctxs - 1)), dma((slots, ctxs - 1)),
            dma((slots, ctxs - 1)), dma((slots, ctxs - 1)),
            dma((slots, 3)), dma((slots, 3)),
            dma((ctxs - 1,)), dma((ctxs - 1,)),
            dma((ctxs - 1,)), dma((ctxs - 1,)),
            dma((ctxs - 1,)), dma((ctxs - 1,)),
            dma((2, slots, ctxs)), dma((2, slots, ctxs)),
            dma((2, slots, ctxs)), dma((2, slots, ctxs)),
            dma((2 * ncols, 2)), dma((2 * ncols, 2)),
            dma((2 * ncols,)), dma((2 * ncols,)),
        ],
        compiler_params=pltpu.CompilerParams(
            collective_id=0, has_side_effects=True, vmem_limit_bytes=62 * 2**20),
        cost_estimate=pl.CostEstimate(
            flops=8 * ctxs * block * key_count * hg + 4 * block * hg * width,
            bytes_accessed=2 * (2 * key_count * hg + hg * width),
            transcendentals=2 * ctxs * block * key_count * hg // HD),
        name="attention",
    )(queries, keys, values, kept_rows, out_weight)


def solution(mesh):
    heads, ctxs = mesh.shape["head"], mesh.shape["ctx"]

    def shards(queries, keys, values, kept_rows, out_weight):
        rows = queries.shape[0]
        if heads == 4 and ctxs == 4 and rows == 32 and keys.shape[1] == 12 * HD:
            return fused_shards(ctxs, queries, keys, values, kept_rows, out_weight)
        return general_shards(queries, keys, values, kept_rows, out_weight)

    placed = (
        P(("abl", "head", "ctx"), None),
        P(("abl", "ctx"), "head"),
        P(("abl", "ctx"), "head"),
        P(("abl", "ctx")),
        P("head", None),
    )
    return jax.shard_map(
        shards,
        mesh=mesh,
        in_specs=placed,
        out_specs=P(("abl", "head", "ctx"), None),
        check_vma=False,
    )
```

```python
import functools
import math

import jax
import jax.numpy as jnp
from jax import lax
from jax.experimental import pallas as pl
from jax.experimental.pallas import tpu as pltpu
from jax.sharding import PartitionSpec as P

HD = 128
KC = 256
AHEAD = 2
DIRECT = 3
MESH = pl.DeviceIdType.MESH
SCALE2 = math.log2(math.e) / math.sqrt(HD)


def general_shards(queries, keys, values, kept_rows, out_weight):
    score_scale = 1.0 / math.sqrt(HD)
    local_heads = keys.shape[1] // HD
    key_count = keys.shape[0]
    key_heads = keys.reshape(key_count, local_heads, HD)
    value_heads = values.reshape(key_count, local_heads, HD)
    visible = jnp.repeat(kept_rows, 128) > 0
    query_block = lax.all_to_all(queries, "head", split_axis=1, concat_axis=0, tiled=True)
    all_queries = lax.all_gather(query_block, "ctx", axis=0, tiled=True)
    row_count = all_queries.shape[0]
    shaped = all_queries.reshape(row_count, local_heads, HD)
    scores = (
        jnp.einsum("qhd,khd->hqk", shaped, key_heads, preferred_element_type=jnp.float32)
        * score_scale
    )
    scores = jnp.where(visible[None, None, :], scores, -jnp.inf)
    running = jnp.max(scores, axis=-1)
    softened = jnp.exp(scores - running[..., None])
    normal_sum = jnp.sum(softened, axis=-1)
    mixed = jnp.einsum(
        "hqk,khd->qhd",
        softened.astype(jnp.bfloat16),
        value_heads,
        preferred_element_type=jnp.float32,
    )
    summed = mixed.reshape(row_count, local_heads * HD)
    highest = lax.pmax(running, "ctx")
    rescale = jnp.exp(running - highest)
    summed = summed * jnp.repeat(rescale.T, HD, axis=1)
    normal_sum = normal_sum * rescale
    summed, normal_sum = (
        lax.psum_scatter(
            summed.astype(jnp.bfloat16), "ctx", scatter_dimension=0, tiled=True
        ).astype(jnp.float32),
        lax.psum_scatter(
            normal_sum.astype(jnp.bfloat16), "ctx", scatter_dimension=1, tiled=True
        ).astype(jnp.float32),
    )
    attended = (summed / jnp.repeat(normal_sum.T, HD, axis=1)).astype(jnp.bfloat16)
    return lax.psum_scatter(
        jnp.dot(attended, out_weight, preferred_element_type=jnp.float32).astype(jnp.bfloat16),
        "head",
        scatter_dimension=0,
        tiled=True,
    )


def kernel(
    q_hbm, k_hbm, v_hbm, kept_ref, w_hbm, out_ref,
    kbuf, vbuf, wbuf, qbuf, abuf, sbuf, rbuf, srbuf, dbuf, dlog, ubuf, ulog, bias, att, pbuf, sib, xsend, xrecv,
    score_ref, prob_ref, top_ref, early,
    kv_sem, w_sem, own_sem, up_s, up_r, dn_s, dn_r, a2a_s, a2a_r, ag_s, ag_r, rs_s, rs_r, st_s, st_r,
    pd_s, pd_r, pu_s, pu_r, sib_s, sib_r, x_s, x_r,
):
    heads, ctxs = 4, qbuf.shape[1]
    groups, _, block, cw = qbuf.shape
    rows = q_hbm.shape[0]
    hg = groups * cw
    per = cw // HD
    ncols, _, _, nw = pbuf.shape
    last = ctxs - 1
    merged = groups - DIRECT
    h = lax.axis_index("head")
    c = lax.axis_index("ctx")

    def kv_copies(g):
        cols = pl.ds(pl.multiple_of(g * cw, cw), cw)
        return (
            pltpu.make_async_copy(k_hbm.at[:, cols], kbuf.at[g], kv_sem.at[0, g]),
            pltpu.make_async_copy(v_hbm.at[:, cols], vbuf.at[g], kv_sem.at[1, g]),
        )

    def w_copy(n):
        cols = pl.ds(pl.multiple_of(n * nw, nw), nw)
        return pltpu.make_async_copy(w_hbm.at[:, cols], wbuf.at[n], w_sem.at[n])

    def a2a(g, d, sender, target):
        return pltpu.make_async_remote_copy(
            src_ref=q_hbm.at[:, pl.ds(pl.multiple_of(target * hg + g * cw, cw), cw)],
            dst_ref=qbuf.at[g, c, pl.ds(pl.multiple_of(sender * rows, rows), rows), :],
            send_sem=a2a_s.at[g, d - 1], recv_sem=a2a_r.at[g, d - 1],
            device_id={"head": target}, device_id_type=MESH)

    def own_copy(g):
        return pltpu.make_async_copy(
            q_hbm.at[:, pl.ds(pl.multiple_of(h * hg + g * cw, cw), cw)],
            qbuf.at[g, c, pl.ds(pl.multiple_of(h * rows, rows), rows), :], own_sem.at[g])

    def gather(g, d, sender, target):
        return pltpu.make_async_remote_copy(
            src_ref=qbuf.at[g, sender], dst_ref=qbuf.at[g, sender],
            send_sem=ag_s.at[g, d - 1], recv_sem=ag_r.at[g, d - 1],
            device_id={"ctx": target}, device_id_type=MESH)

    def up(g, k, part):
        return pltpu.make_async_remote_copy(
            src_ref=qbuf.at[g, part], dst_ref=qbuf.at[g, part],
            send_sem=up_s.at[g, k], recv_sem=up_r.at[g, k],
            device_id={"ctx": lax.rem(c + 1, ctxs)}, device_id_type=MESH)

    def down(g, k, part):
        return pltpu.make_async_remote_copy(
            src_ref=qbuf.at[g, part], dst_ref=qbuf.at[g, part],
            send_sem=dn_s.at[g, k], recv_sem=dn_r.at[g, k],
            device_id={"ctx": lax.rem(c + ctxs - 1, ctxs)}, device_id_type=MESH)

    def exchanged(g):
        own_copy(g).wait()
        for d in range(1, heads):
            a2a(g, d, lax.rem(h + heads - d, heads), h).wait_recv()

    def hop(g, k):
        @pl.when(jnp.logical_and(c < last, c >= k))
        def _():
            if k:
                up(g, k - 1, c - k).wait_recv()
            up(g, k, c - k).start()

        @pl.when(jnp.logical_and(c > 0, c + k <= last))
        def _():
            if k:
                down(g, k - 1, c + k).wait_recv()
            down(g, k, c + k).start()

    def stage(s):
        for k in range(last):
            g = s - k
            inside = jnp.logical_and(g >= AHEAD, g < groups)

            @pl.when(inside)
            def _():
                if k == 0:
                    exchanged(g)
                hop(g, k)

    def scatter(g, d, target):
        return (
            pltpu.make_async_remote_copy(
                src_ref=abuf.at[g, target], dst_ref=rbuf.at[g - merged, d - 1],
                send_sem=rs_s.at[g - merged, d - 1], recv_sem=rs_r.at[g - merged, d - 1],
                device_id={"ctx": target}, device_id_type=MESH),
            pltpu.make_async_remote_copy(
                src_ref=sbuf.at[g, target], dst_ref=srbuf.at[g - merged, d - 1],
                send_sem=st_s.at[g - merged, d - 1], recv_sem=st_r.at[g - merged, d - 1],
                device_id={"ctx": target}, device_id_type=MESH),
        )

    def part_down(g, b):
        target = lax.rem(c + ctxs - 1, ctxs)
        return (
            pltpu.make_async_remote_copy(
                src_ref=sbuf.at[g, b], dst_ref=dlog.at[g, b],
                send_sem=pd_s.at[1, g, b], recv_sem=pd_r.at[1, g, b],
                device_id={"ctx": target}, device_id_type=MESH),
            pltpu.make_async_remote_copy(
                src_ref=abuf.at[g, b], dst_ref=dbuf.at[g, b],
                send_sem=pd_s.at[0, g, b], recv_sem=pd_r.at[0, g, b],
                device_id={"ctx": target}, device_id_type=MESH),
        )

    def part_up(g, b):
        target = lax.rem(c + 1, ctxs)
        return (
            pltpu.make_async_remote_copy(
                src_ref=sbuf.at[g, b], dst_ref=ulog.at[g, b],
                send_sem=pu_s.at[1, g, b], recv_sem=pu_r.at[1, g, b],
                device_id={"ctx": target}, device_id_type=MESH),
            pltpu.make_async_remote_copy(
                src_ref=abuf.at[g, b], dst_ref=ubuf.at[g, b],
                send_sem=pu_s.at[0, g, b], recv_sem=pu_r.at[0, g, b],
                device_id={"ctx": target}, device_id_type=MESH),
        )

    def merge(g, b, part, log):
        mine, other = sbuf[g, b], log[g, b]
        top = jnp.maximum(mine, other)
        weights = jnp.exp2(mine - top), jnp.exp2(other - top)
        total = weights[0] + weights[1]
        sbuf[g, b] = top + jnp.log2(total)
        columns = jnp.concatenate(
            [weights[0] / total, weights[1] / total, jnp.zeros((HD - 16, block), jnp.float32)], axis=0).T
        for j in range(per):
            cols = slice(j * HD, (j + 1) * HD)
            abuf[g, b, :, cols] = (
                columns[:, j:j + 1] * abuf[g, b, :, cols].astype(jnp.float32)
                + columns[:, 8 + j:9 + j] * part[g, b, :, cols].astype(jnp.float32)
            ).astype(jnp.bfloat16)

    def part_stage(g, s):
        @pl.when(c == last - s)
        def _():
            for b in range(last - s):
                if s:
                    for copy in part_down(g, b):
                        copy.wait_recv()
                    merge(g, b, dbuf, dlog)
                for copy in part_down(g, b):
                    copy.start()

        @pl.when(c == s)
        def _():
            for b in range(last, s, -1):
                if s:
                    for copy in part_up(g, b):
                        copy.wait_recv()
                    merge(g, b, ubuf, ulog)
                for copy in part_up(g, b):
                    copy.start()

    def part_final(g):
        @pl.when(c < last)
        def _():
            for copy in part_down(g, c):
                copy.wait_recv()
            merge(g, c, dbuf, dlog)

        @pl.when(c > 0)
        def _():
            for copy in part_up(g, c):
                copy.wait_recv()
            merge(g, c, ubuf, ulog)

        att[g] = abuf[g, c]

    def direct_final(g):
        for d in range(1, ctxs):
            for copy in scatter(g, d, lax.rem(c + d, ctxs)):
                copy.wait_recv()
        logs = jnp.concatenate(
            [sbuf[g, c]] + [srbuf[g - merged, d] for d in range(ctxs - 1)]
            + [jnp.zeros((HD - 8 * ctxs, block), jnp.float32)], axis=0).T
        for j in range(per):
            cols = slice(j * HD, (j + 1) * HD)
            own = [logs[:, 8 * i + j:8 * i + j + 1] for i in range(ctxs)]
            top = functools.reduce(jnp.maximum, own)
            weights = [jnp.exp2(x - top) for x in own]
            total = functools.reduce(jnp.add, weights)
            parts = [abuf[g, c, :, cols]] + [rbuf[g - merged, d, :, cols] for d in range(ctxs - 1)]
            value = functools.reduce(jnp.add, [w * x.astype(jnp.float32) for w, x in zip(weights, parts)])
            att[g, :, cols] = (value / total).astype(jnp.bfloat16)

    sibling = h + 1 - 2 * lax.rem(h, 2)
    across = lax.rem(h + 2, 4)
    diagonal = lax.rem(sibling + 2, 4)

    def to_sibling(n, i):
        return pltpu.make_async_remote_copy(
            src_ref=pbuf.at[n, sibling if i else diagonal], dst_ref=sib.at[n, i],
            send_sem=sib_s.at[n, i], recv_sem=sib_r.at[n, i],
            device_id={"head": sibling}, device_id_type=MESH)

    def to_across(n):
        return pltpu.make_async_remote_copy(
            src_ref=xsend.at[n], dst_ref=xrecv.at[n],
            send_sem=x_s.at[n], recv_sem=x_r.at[n],
            device_id={"head": across}, device_id_type=MESH)

    def send_across(n):
        to_sibling(n, 0).wait_recv()
        xsend[n] = (pbuf[n, across].astype(jnp.float32) + sib[n, 0].astype(jnp.float32)).astype(jnp.bfloat16)
        to_across(n).start()

    barrier = pltpu.get_barrier_semaphore()
    for d in range(1, heads):
        pl.semaphore_signal(barrier, inc=1, device_id={"head": lax.rem(h + d, heads)}, device_id_type=MESH)
    for d in range(1, ctxs):
        pl.semaphore_signal(barrier, inc=1, device_id={"ctx": lax.rem(c + d, ctxs)}, device_id_type=MESH)

    @pl.loop(0, groups)
    def _(g):
        for copy in kv_copies(g):
            copy.start()

    pl.semaphore_wait(barrier, heads + ctxs - 2)

    @pl.loop(0, groups)
    def _(g):
        for d in (2, 1, 3):
            a2a(g, d, h, lax.rem(h + d, heads)).start()
        own_copy(g).start()

    @pl.loop(0, ncols)
    def _(n):
        w_copy(n).start()

    for i in range(kept_ref.shape[0]):
        bias[:, i * 128:(i + 1) * 128] = jnp.full(
            (8, 128), jnp.where(kept_ref[i] > 0, 0.0, -jnp.inf), jnp.float32)

    exchanged(0)
    for d in (2, 1, 3):
        gather(0, d, c, lax.rem(c + d, ctxs)).start()
    exchanged(AHEAD)
    hop(AHEAD, 0)
    for g in range(1, AHEAD):
        exchanged(g)
        for d in (2, 1, 3):
            gather(g, d, c, lax.rem(c + d, ctxs)).start()

    ones = jnp.ones((kbuf.shape[1] // 2, HD), jnp.bfloat16)
    lane = lax.broadcasted_iota(jnp.int32, (2 * block, HD), 1)

    @pl.loop(0, groups)
    def _(g):
        @pl.when(g < AHEAD)
        def _():
            for d in range(1, ctxs):
                gather(g, d, lax.rem(c + ctxs - d, ctxs), c).wait_recv()

        @pl.when(jnp.logical_and(g >= AHEAD, c == last))
        def _():
            for k in range(last):
                up(g, k, last - 1 - k).wait_recv()

        @pl.when(jnp.logical_and(g >= AHEAD, c == 0))
        def _():
            for k in range(last):
                down(g, k, 1 + k).wait_recv()

        for copy in kv_copies(g):
            copy.wait()
        stage(g + 3)
        stats = [jnp.zeros((2 * block, HD), jnp.float32) for _ in range(ctxs // 2)]
        units = [(j, t) for j in range(per) for t in range(ctxs // 2)]
        key_count = kbuf.shape[1]
        chunks = key_count // KC
        tops = {}
        for u in range(len(units) + 1):
            mixed = None
            if u < len(units):
                j, t = units[u]
                query = qbuf[g, 2 * t:2 * t + 2, :, j * HD:(j + 1) * HD].reshape(2 * block, HD)
                running = None
            for kc in range(chunks):
                keys = slice(kc * KC, (kc + 1) * KC)
                if u < len(units):
                    scores = lax.dot_general(
                        query, kbuf[g, keys, j * HD:(j + 1) * HD], (((1,), (1,)), ((), ())),
                        preferred_element_type=jnp.float32) + bias[0:1, keys]
                    score_ref[u % 2, :, keys] = scores
                    for i in range(KC // HD):
                        piece = scores[:, i * HD:(i + 1) * HD]
                        running = piece if running is None else jnp.maximum(running, piece)
                if u > 0:
                    pj, pt = units[u - 1]
                    for i in range(KC // HD):
                        cols = slice(kc * KC + i * HD, kc * KC + (i + 1) * HD)
                        prob_ref[(u - 1) % 2, :, cols] = jnp.exp2(
                            (score_ref[(u - 1) % 2, :, cols] - top_ref[(u - 1) % 2]) * SCALE2
                        ).astype(jnp.bfloat16)
                    if (kc + 1) % (chunks // 2) == 0:
                        span = slice((kc + 1) * KC - key_count // 2, (kc + 1) * KC)
                        value = jnp.concatenate([vbuf[g, span, pj * HD:(pj + 1) * HD], ones], axis=1)
                        part = jnp.dot(
                            prob_ref[(u - 1) % 2, :, span], value, preferred_element_type=jnp.float32)
                        mixed = part if mixed is None else mixed + part
            if u > 0:
                normal = mixed[:, HD:]
                abuf[g, 2 * pt:2 * pt + 2, :, pj * HD:(pj + 1) * HD] = (
                    (mixed[:, :HD] / normal).astype(jnp.bfloat16).reshape(2, block, HD))
                stats[pt] = jnp.where(
                    lane == pj, top_ref[(u - 1) % 2] * SCALE2 + jnp.log2(normal), stats[pt])
            if u < len(units):
                top_ref[u % 2] = jnp.broadcast_to(
                    jnp.max(running, axis=1, keepdims=True), (2 * block, HD))
        for t in range(ctxs // 2):
            for u in range(2):
                sbuf[g, 2 * t + u] = stats[t][u * block:(u + 1) * block].T[0:8, :]

        @pl.when(g < merged)
        def _():
            part_stage(g, 0)

        @pl.when(g >= merged)
        def _():
            for d in (2, 1, 3):
                for copy in scatter(g, d, lax.rem(c + d, ctxs)):
                    copy.start()

        @pl.when(jnp.logical_and(g >= 2, g < merged + 2))
        def _():
            part_stage(g - 2, 1)

        @pl.when(jnp.logical_and(g >= 3, g < merged + 3))
        def _():
            part_stage(g - 3, 2)

        @pl.when(jnp.logical_and(g >= 4, g < merged + 4))
        def _():
            part_final(g - 4)

    for g in range(merged):
        if g + 2 >= groups:
            part_stage(g, 1)
        if g + 3 >= groups:
            part_stage(g, 2)
    for g in range(merged):
        if g + 4 >= groups:
            part_final(g)
    for g in range(merged, groups - 1):
        direct_final(g)

    @pl.loop(0, ncols)
    def _(n):
        w_copy(n).wait()
        early[n] = functools.reduce(jnp.add, [
            jnp.dot(att[g], wbuf[n, g * cw:(g + 1) * cw, :], preferred_element_type=jnp.float32)
            for g in range(groups - 1)])

    direct_final(groups - 1)

    @pl.loop(0, ncols)
    def _(n):
        total = early[n] + jnp.dot(
            att[groups - 1], wbuf[n, (groups - 1) * cw:, :], preferred_element_type=jnp.float32)
        pbuf[n] = total.astype(jnp.bfloat16).reshape(heads, rows, nw)
        for i in range(2):
            to_sibling(n, i).start()

        @pl.when(n > 0)
        def _():
            send_across(n - 1)

    send_across(ncols - 1)

    for n in range(ncols):
        to_sibling(n, 1).wait_recv()
        to_across(n).wait_recv()
        out_ref[:, n * nw:(n + 1) * nw] = (
            pbuf[n, h].astype(jnp.float32) + sib[n, 1].astype(jnp.float32)
            + xrecv[n].astype(jnp.float32)).astype(jnp.bfloat16)

    @pl.loop(0, groups)
    def _(g):
        for d in range(1, heads):
            a2a(g, d, h, lax.rem(h + d, heads)).wait_send()
        for k in range(last):
            @pl.when(jnp.logical_and(g >= AHEAD, jnp.logical_and(c < last, c >= k)))
            def _():
                up(g, k, c - k).wait_send()

            @pl.when(jnp.logical_and(g >= AHEAD, jnp.logical_and(c > 0, c + k <= last)))
            def _():
                down(g, k, c + k).wait_send()

        for b in range(ctxs):
            @pl.when(jnp.logical_and(g < merged, b < c))
            def _():
                for copy in part_down(g, b):
                    copy.wait_send()

            @pl.when(jnp.logical_and(g < merged, b > c))
            def _():
                for copy in part_up(g, b):
                    copy.wait_send()

    for d in range(1, ctxs):
        for g in range(AHEAD):
            gather(g, d, c, lax.rem(c + d, ctxs)).wait_send()
        for g in range(merged, groups):
            for copy in scatter(g, d, lax.rem(c + d, ctxs)):
                copy.wait_send()

    @pl.loop(0, ncols)
    def _(n):
        to_sibling(n, 0).wait_send()
        to_sibling(n, 1).wait_send()
        to_across(n).wait_send()


def fused_shards(ctxs, queries, keys, values, kept_rows, out_weight):
    rows, width = queries.shape
    key_count, hg = keys.shape
    cw = 2 * HD
    groups = hg // cw
    block = 4 * rows
    nw = 1024
    ncols = width // nw
    bf, f32 = jnp.bfloat16, jnp.float32
    dma = pltpu.SemaphoreType.DMA
    vmem = pl.BlockSpec(memory_space=pltpu.VMEM)
    hbm = pl.BlockSpec(memory_space=pl.ANY)
    return pl.pallas_call(
        kernel,
        out_shape=jax.ShapeDtypeStruct((rows, width), bf),
        in_specs=[hbm, hbm, hbm, pl.BlockSpec(memory_space=pltpu.SMEM), hbm],
        out_specs=vmem,
        scratch_shapes=[
            pltpu.VMEM((groups, key_count, cw), bf),
            pltpu.VMEM((groups, key_count, cw), bf),
            pltpu.VMEM((ncols, hg, nw), bf),
            pltpu.VMEM((groups, ctxs, block, cw), bf),
            pltpu.VMEM((groups, ctxs, block, cw), bf),
            pltpu.VMEM((groups, ctxs, 8, block), f32),
            pltpu.VMEM((DIRECT, ctxs - 1, block, cw), bf),
            pltpu.VMEM((DIRECT, ctxs - 1, 8, block), f32),
            pltpu.VMEM((groups, ctxs, block, cw), bf),
            pltpu.VMEM((groups, ctxs, 8, block), f32),
            pltpu.VMEM((groups, ctxs, block, cw), bf),
            pltpu.VMEM((groups, ctxs, 8, block), f32),
            pltpu.VMEM((8, key_count), f32),
            pltpu.VMEM((groups, block, cw), bf),
            pltpu.VMEM((ncols, 4, rows, nw), bf),
            pltpu.VMEM((ncols, 2, rows, nw), bf),
            pltpu.VMEM((ncols, rows, nw), bf),
            pltpu.VMEM((ncols, rows, nw), bf),
            pltpu.VMEM((2, 2 * block, key_count), f32),
            pltpu.VMEM((2, 2 * block, key_count), bf),
            pltpu.VMEM((2, 2 * block, HD), f32),
            pltpu.VMEM((ncols, block, nw), f32),
            dma((2, groups)), dma((ncols,)), dma((groups,)),
            dma((groups, ctxs - 1)), dma((groups, ctxs - 1)),
            dma((groups, ctxs - 1)), dma((groups, ctxs - 1)),
            dma((groups, 3)), dma((groups, 3)),
            dma((AHEAD, ctxs - 1)), dma((AHEAD, ctxs - 1)),
            dma((DIRECT, ctxs - 1)), dma((DIRECT, ctxs - 1)),
            dma((DIRECT, ctxs - 1)), dma((DIRECT, ctxs - 1)),
            dma((2, groups, ctxs)), dma((2, groups, ctxs)),
            dma((2, groups, ctxs)), dma((2, groups, ctxs)),
            dma((ncols, 2)), dma((ncols, 2)),
            dma((ncols,)), dma((ncols,)),
        ],
        compiler_params=pltpu.CompilerParams(
            collective_id=0, has_side_effects=True, vmem_limit_bytes=62 * 2**20),
        cost_estimate=pl.CostEstimate(
            flops=4 * ctxs * block * key_count * hg + 2 * block * hg * width,
            bytes_accessed=2 * (2 * key_count * hg + hg * width),
            transcendentals=ctxs * block * key_count * hg // HD),
        name="attention",
    )(queries, keys, values, kept_rows, out_weight)


def solution(mesh):
    heads, ctxs = mesh.shape["head"], mesh.shape["ctx"]

    def shards(queries, keys, values, kept_rows, out_weight):
        rows = queries.shape[0]
        if heads == 4 and ctxs == 4 and rows == 32 and keys.shape[1] == 12 * HD:
            return fused_shards(ctxs, queries, keys, values, kept_rows, out_weight)
        return general_shards(queries, keys, values, kept_rows, out_weight)

    placed = (
        P(("abl", "head", "ctx"), None),
        P(("abl", "ctx"), "head"),
        P(("abl", "ctx"), "head"),
        P(("abl", "ctx")),
        P("head", None),
    )
    return jax.shard_map(
        shards,
        mesh=mesh,
        in_specs=placed,
        out_specs=P(("abl", "head", "ctx"), None),
        check_vma=False,
    )
```

```python
import functools
import math

import jax
import jax.numpy as jnp
from jax import lax
from jax.experimental import pallas as pl
from jax.experimental.pallas import tpu as pltpu
from jax.sharding import PartitionSpec as P

HD = 128
KC = 256
AHEAD = 1
DIRECT = 1
MESH = pl.DeviceIdType.MESH
SCALE2 = math.log2(math.e) / math.sqrt(HD)


def general_shards(queries, keys, values, kept_rows, out_weight):
    score_scale = 1.0 / math.sqrt(HD)
    local_heads = keys.shape[1] // HD
    key_count = keys.shape[0]
    key_heads = keys.reshape(key_count, local_heads, HD)
    value_heads = values.reshape(key_count, local_heads, HD)
    visible = jnp.repeat(kept_rows, 128) > 0
    query_block = lax.all_to_all(queries, "head", split_axis=1, concat_axis=0, tiled=True)
    all_queries = lax.all_gather(query_block, "ctx", axis=0, tiled=True)
    row_count = all_queries.shape[0]
    shaped = all_queries.reshape(row_count, local_heads, HD)
    scores = (
        jnp.einsum("qhd,khd->hqk", shaped, key_heads, preferred_element_type=jnp.float32)
        * score_scale
    )
    scores = jnp.where(visible[None, None, :], scores, -jnp.inf)
    running = jnp.max(scores, axis=-1)
    softened = jnp.exp(scores - running[..., None])
    normal_sum = jnp.sum(softened, axis=-1)
    mixed = jnp.einsum(
        "hqk,khd->qhd",
        softened.astype(jnp.bfloat16),
        value_heads,
        preferred_element_type=jnp.float32,
    )
    summed = mixed.reshape(row_count, local_heads * HD)
    highest = lax.pmax(running, "ctx")
    rescale = jnp.exp(running - highest)
    summed = summed * jnp.repeat(rescale.T, HD, axis=1)
    normal_sum = normal_sum * rescale
    summed, normal_sum = (
        lax.psum_scatter(
            summed.astype(jnp.bfloat16), "ctx", scatter_dimension=0, tiled=True
        ).astype(jnp.float32),
        lax.psum_scatter(
            normal_sum.astype(jnp.bfloat16), "ctx", scatter_dimension=1, tiled=True
        ).astype(jnp.float32),
    )
    attended = (summed / jnp.repeat(normal_sum.T, HD, axis=1)).astype(jnp.bfloat16)
    return lax.psum_scatter(
        jnp.dot(attended, out_weight, preferred_element_type=jnp.float32).astype(jnp.bfloat16),
        "head",
        scatter_dimension=0,
        tiled=True,
    )


def kernel(
    q_hbm, k_hbm, v_hbm, kept_ref, w_hbm, out_ref,
    kbuf, vbuf, wbuf, qbuf, abuf, sbuf, rbuf, srbuf, dbuf, dlog, ubuf, ulog, bias, att, pbuf, sib, xsend, xrecv,
    score_ref, prob_ref, top_ref, early,
    kv_sem, w_sem, own_sem, up_s, up_r, dn_s, dn_r, a2a_s, a2a_r, ag_s, ag_r, rs_s, rs_r, st_s, st_r,
    pd_s, pd_r, pu_s, pu_r, sib_s, sib_r, x_s, x_r,
):
    heads, ctxs = 4, qbuf.shape[1]
    groups, _, block, cw = qbuf.shape
    rows = q_hbm.shape[0]
    hg = groups * cw
    per = cw // HD
    ncols, _, _, nw = pbuf.shape
    last = ctxs - 1
    merged = groups - DIRECT
    h = lax.axis_index("head")
    c = lax.axis_index("ctx")

    def kv_copies(g):
        cols = pl.ds(pl.multiple_of(g * cw, cw), cw)
        return (
            pltpu.make_async_copy(k_hbm.at[:, cols], kbuf.at[g], kv_sem.at[0, g]),
            pltpu.make_async_copy(v_hbm.at[:, cols], vbuf.at[g], kv_sem.at[1, g]),
        )

    def w_copy(n):
        cols = pl.ds(pl.multiple_of(n * nw, nw), nw)
        return pltpu.make_async_copy(w_hbm.at[:, cols], wbuf.at[n], w_sem.at[n])

    def a2a(g, d, sender, target):
        return pltpu.make_async_remote_copy(
            src_ref=q_hbm.at[:, pl.ds(pl.multiple_of(target * hg + g * cw, cw), cw)],
            dst_ref=qbuf.at[g, c, pl.ds(pl.multiple_of(sender * rows, rows), rows), :],
            send_sem=a2a_s.at[g, d - 1], recv_sem=a2a_r.at[g, d - 1],
            device_id={"head": target}, device_id_type=MESH)

    def own_copy(g):
        return pltpu.make_async_copy(
            q_hbm.at[:, pl.ds(pl.multiple_of(h * hg + g * cw, cw), cw)],
            qbuf.at[g, c, pl.ds(pl.multiple_of(h * rows, rows), rows), :], own_sem.at[g])

    def gather(g, d, sender, target):
        return pltpu.make_async_remote_copy(
            src_ref=qbuf.at[g, sender], dst_ref=qbuf.at[g, sender],
            send_sem=ag_s.at[g, d - 1], recv_sem=ag_r.at[g, d - 1],
            device_id={"ctx": target}, device_id_type=MESH)

    def up(g, k, part):
        return pltpu.make_async_remote_copy(
            src_ref=qbuf.at[g, part], dst_ref=qbuf.at[g, part],
            send_sem=up_s.at[g, k], recv_sem=up_r.at[g, k],
            device_id={"ctx": lax.rem(c + 1, ctxs)}, device_id_type=MESH)

    def down(g, k, part):
        return pltpu.make_async_remote_copy(
            src_ref=qbuf.at[g, part], dst_ref=qbuf.at[g, part],
            send_sem=dn_s.at[g, k], recv_sem=dn_r.at[g, k],
            device_id={"ctx": lax.rem(c + ctxs - 1, ctxs)}, device_id_type=MESH)

    def exchanged(g):
        own_copy(g).wait()
        for d in range(1, heads):
            a2a(g, d, lax.rem(h + heads - d, heads), h).wait_recv()

    def hop(g, k):
        @pl.when(jnp.logical_and(c < last, c >= k))
        def _():
            if k:
                up(g, k - 1, c - k).wait_recv()
            up(g, k, c - k).start()

        @pl.when(jnp.logical_and(c > 0, c + k <= last))
        def _():
            if k:
                down(g, k - 1, c + k).wait_recv()
            down(g, k, c + k).start()

    def stage(s):
        for k in range(last):
            g = s - k
            inside = jnp.logical_and(g >= AHEAD, g < groups)

            @pl.when(inside)
            def _():
                if k == 0:
                    exchanged(g)
                hop(g, k)

    def scatter(g, d, target):
        return (
            pltpu.make_async_remote_copy(
                src_ref=abuf.at[g, target], dst_ref=rbuf.at[g - merged, d - 1],
                send_sem=rs_s.at[g - merged, d - 1], recv_sem=rs_r.at[g - merged, d - 1],
                device_id={"ctx": target}, device_id_type=MESH),
            pltpu.make_async_remote_copy(
                src_ref=sbuf.at[g, target], dst_ref=srbuf.at[g - merged, d - 1],
                send_sem=st_s.at[g - merged, d - 1], recv_sem=st_r.at[g - merged, d - 1],
                device_id={"ctx": target}, device_id_type=MESH),
        )

    def part_down(g, b):
        target = lax.rem(c + ctxs - 1, ctxs)
        return (
            pltpu.make_async_remote_copy(
                src_ref=sbuf.at[g, b], dst_ref=dlog.at[g, b],
                send_sem=pd_s.at[1, g, b], recv_sem=pd_r.at[1, g, b],
                device_id={"ctx": target}, device_id_type=MESH),
            pltpu.make_async_remote_copy(
                src_ref=abuf.at[g, b], dst_ref=dbuf.at[g, b],
                send_sem=pd_s.at[0, g, b], recv_sem=pd_r.at[0, g, b],
                device_id={"ctx": target}, device_id_type=MESH),
        )

    def part_up(g, b):
        target = lax.rem(c + 1, ctxs)
        return (
            pltpu.make_async_remote_copy(
                src_ref=sbuf.at[g, b], dst_ref=ulog.at[g, b],
                send_sem=pu_s.at[1, g, b], recv_sem=pu_r.at[1, g, b],
                device_id={"ctx": target}, device_id_type=MESH),
            pltpu.make_async_remote_copy(
                src_ref=abuf.at[g, b], dst_ref=ubuf.at[g, b],
                send_sem=pu_s.at[0, g, b], recv_sem=pu_r.at[0, g, b],
                device_id={"ctx": target}, device_id_type=MESH),
        )

    def merge(g, b, part, log):
        mine, other = sbuf[g, b], log[g, b]
        top = jnp.maximum(mine, other)
        weights = jnp.exp2(mine - top), jnp.exp2(other - top)
        total = weights[0] + weights[1]
        sbuf[g, b] = top + jnp.log2(total)
        columns = jnp.concatenate(
            [weights[0] / total, weights[1] / total, jnp.zeros((HD - 16, block), jnp.float32)], axis=0).T
        for j in range(per):
            cols = slice(j * HD, (j + 1) * HD)
            abuf[g, b, :, cols] = (
                columns[:, j:j + 1] * abuf[g, b, :, cols].astype(jnp.float32)
                + columns[:, 8 + j:9 + j] * part[g, b, :, cols].astype(jnp.float32)
            ).astype(jnp.bfloat16)

    def part_stage(g, s):
        @pl.when(c == last - s)
        def _():
            for b in range(last - s):
                if s:
                    for copy in part_down(g, b):
                        copy.wait_recv()
                    merge(g, b, dbuf, dlog)
                for copy in part_down(g, b):
                    copy.start()

        @pl.when(c == s)
        def _():
            for b in range(last, s, -1):
                if s:
                    for copy in part_up(g, b):
                        copy.wait_recv()
                    merge(g, b, ubuf, ulog)
                for copy in part_up(g, b):
                    copy.start()

    def part_final(g):
        @pl.when(c < last)
        def _():
            for copy in part_down(g, c):
                copy.wait_recv()
            merge(g, c, dbuf, dlog)

        @pl.when(c > 0)
        def _():
            for copy in part_up(g, c):
                copy.wait_recv()
            merge(g, c, ubuf, ulog)

        att[g] = abuf[g, c]

    def direct_final(g):
        for d in range(1, ctxs):
            for copy in scatter(g, d, lax.rem(c + d, ctxs)):
                copy.wait_recv()
        logs = jnp.concatenate(
            [sbuf[g, c]] + [srbuf[g - merged, d] for d in range(ctxs - 1)]
            + [jnp.zeros((HD - 8 * ctxs, block), jnp.float32)], axis=0).T
        for j in range(per):
            cols = slice(j * HD, (j + 1) * HD)
            own = [logs[:, 8 * i + j:8 * i + j + 1] for i in range(ctxs)]
            top = functools.reduce(jnp.maximum, own)
            weights = [jnp.exp2(x - top) for x in own]
            total = functools.reduce(jnp.add, weights)
            parts = [abuf[g, c, :, cols]] + [rbuf[g - merged, d, :, cols] for d in range(ctxs - 1)]
            value = functools.reduce(jnp.add, [w * x.astype(jnp.float32) for w, x in zip(weights, parts)])
            att[g, :, cols] = (value / total).astype(jnp.bfloat16)

    sibling = h + 1 - 2 * lax.rem(h, 2)
    across = lax.rem(h + 2, 4)
    diagonal = lax.rem(sibling + 2, 4)

    def to_sibling(n, i):
        return pltpu.make_async_remote_copy(
            src_ref=pbuf.at[n, sibling if i else diagonal], dst_ref=sib.at[n, i],
            send_sem=sib_s.at[n, i], recv_sem=sib_r.at[n, i],
            device_id={"head": sibling}, device_id_type=MESH)

    def to_across(n):
        return pltpu.make_async_remote_copy(
            src_ref=xsend.at[n], dst_ref=xrecv.at[n],
            send_sem=x_s.at[n], recv_sem=x_r.at[n],
            device_id={"head": across}, device_id_type=MESH)

    def send_across(n):
        to_sibling(n, 0).wait_recv()
        xsend[n] = (pbuf[n, across].astype(jnp.float32) + sib[n, 0].astype(jnp.float32)).astype(jnp.bfloat16)
        to_across(n).start()

    barrier = pltpu.get_barrier_semaphore()
    for d in range(1, heads):
        pl.semaphore_signal(barrier, inc=1, device_id={"head": lax.rem(h + d, heads)}, device_id_type=MESH)
    for d in range(1, ctxs):
        pl.semaphore_signal(barrier, inc=1, device_id={"ctx": lax.rem(c + d, ctxs)}, device_id_type=MESH)

    @pl.loop(0, groups)
    def _(g):
        for copy in kv_copies(g):
            copy.start()

    pl.semaphore_wait(barrier, heads + ctxs - 2)

    @pl.loop(0, groups)
    def _(g):
        for d in (2, 1, 3):
            a2a(g, d, h, lax.rem(h + d, heads)).start()
        own_copy(g).start()

    @pl.loop(0, ncols)
    def _(n):
        w_copy(n).start()

    for i in range(kept_ref.shape[0]):
        bias[:, i * 128:(i + 1) * 128] = jnp.full(
            (8, 128), jnp.where(kept_ref[i] > 0, 0.0, -jnp.inf), jnp.float32)

    exchanged(0)
    for d in (2, 1, 3):
        gather(0, d, c, lax.rem(c + d, ctxs)).start()
    exchanged(AHEAD)
    hop(AHEAD, 0)
    stage(AHEAD + 1)
    for g in range(1, AHEAD):
        exchanged(g)
        for d in (2, 1, 3):
            gather(g, d, c, lax.rem(c + d, ctxs)).start()

    ones = jnp.ones((kbuf.shape[1] // 2, HD), jnp.bfloat16)
    lane = lax.broadcasted_iota(jnp.int32, (2 * block, HD), 1)

    @pl.loop(0, groups)
    def _(g):
        @pl.when(g < AHEAD)
        def _():
            for d in range(1, ctxs):
                gather(g, d, lax.rem(c + ctxs - d, ctxs), c).wait_recv()

        @pl.when(jnp.logical_and(g >= AHEAD, c == last))
        def _():
            for k in range(last):
                up(g, k, last - 1 - k).wait_recv()

        @pl.when(jnp.logical_and(g >= AHEAD, c == 0))
        def _():
            for k in range(last):
                down(g, k, 1 + k).wait_recv()

        for copy in kv_copies(g):
            copy.wait()
        stage(g + 3)
        stats = [jnp.zeros((2 * block, HD), jnp.float32) for _ in range(ctxs // 2)]
        units = [(j, t) for j in range(per) for t in range(ctxs // 2)]
        key_count = kbuf.shape[1]
        chunks = key_count // KC
        tops = {}
        for u in range(len(units) + 1):
            mixed = None
            if u < len(units):
                j, t = units[u]
                query = qbuf[g, 2 * t:2 * t + 2, :, j * HD:(j + 1) * HD].reshape(2 * block, HD)
                running = None
            for kc in range(chunks):
                keys = slice(kc * KC, (kc + 1) * KC)
                if u < len(units):
                    scores = lax.dot_general(
                        query, kbuf[g, keys, j * HD:(j + 1) * HD], (((1,), (1,)), ((), ())),
                        preferred_element_type=jnp.float32) + bias[0:1, keys]
                    score_ref[u % 2, :, keys] = scores
                    for i in range(KC // HD):
                        piece = scores[:, i * HD:(i + 1) * HD]
                        running = piece if running is None else jnp.maximum(running, piece)
                if u > 0:
                    pj, pt = units[u - 1]
                    for i in range(KC // HD):
                        cols = slice(kc * KC + i * HD, kc * KC + (i + 1) * HD)
                        prob_ref[(u - 1) % 2, :, cols] = jnp.exp2(
                            (score_ref[(u - 1) % 2, :, cols] - top_ref[(u - 1) % 2]) * SCALE2
                        ).astype(jnp.bfloat16)
                    if (kc + 1) % (chunks // 2) == 0:
                        span = slice((kc + 1) * KC - key_count // 2, (kc + 1) * KC)
                        value = jnp.concatenate([vbuf[g, span, pj * HD:(pj + 1) * HD], ones], axis=1)
                        part = jnp.dot(
                            prob_ref[(u - 1) % 2, :, span], value, preferred_element_type=jnp.float32)
                        mixed = part if mixed is None else mixed + part
            if u > 0:
                normal = mixed[:, HD:]
                abuf[g, 2 * pt:2 * pt + 2, :, pj * HD:(pj + 1) * HD] = (
                    (mixed[:, :HD] / normal).astype(jnp.bfloat16).reshape(2, block, HD))
                stats[pt] = jnp.where(
                    lane == pj, top_ref[(u - 1) % 2] * SCALE2 + jnp.log2(normal), stats[pt])
            if u < len(units):
                top_ref[u % 2] = jnp.broadcast_to(
                    jnp.max(running, axis=1, keepdims=True), (2 * block, HD))
        for t in range(ctxs // 2):
            for u in range(2):
                sbuf[g, 2 * t + u] = stats[t][u * block:(u + 1) * block].T[0:8, :]

        @pl.when(g < merged)
        def _():
            part_stage(g, 0)

        @pl.when(jnp.logical_and(g >= 1, g < merged + 1))
        def _():
            part_stage(g - 1, 1)

        @pl.when(jnp.logical_and(g >= 2, g < merged + 2))
        def _():
            part_stage(g - 2, 2)

        @pl.when(g >= merged)
        def _():
            for d in (2, 1, 3):
                for copy in scatter(g, d, lax.rem(c + d, ctxs)):
                    copy.start()

        @pl.when(jnp.logical_and(g >= 3, g < merged + 3))
        def _():
            part_final(g - 3)

    for g in range(merged):
        if g + 2 >= groups:
            part_stage(g, 2)
    for g in range(merged):
        if g + 3 >= groups:
            part_final(g)
    for g in range(merged, groups - 1):
        direct_final(g)

    @pl.loop(0, ncols)
    def _(n):
        w_copy(n).wait()
        early[n] = functools.reduce(jnp.add, [
            jnp.dot(att[g], wbuf[n, g * cw:(g + 1) * cw, :], preferred_element_type=jnp.float32)
            for g in range(groups - 1)])

    direct_final(groups - 1)

    @pl.loop(0, ncols)
    def _(n):
        total = early[n] + jnp.dot(
            att[groups - 1], wbuf[n, (groups - 1) * cw:, :], preferred_element_type=jnp.float32)
        pbuf[n] = total.astype(jnp.bfloat16).reshape(heads, rows, nw)
        for i in range(2):
            to_sibling(n, i).start()

        @pl.when(n > 0)
        def _():
            send_across(n - 1)

    send_across(ncols - 1)

    for n in range(ncols):
        to_sibling(n, 1).wait_recv()
        to_across(n).wait_recv()
        out_ref[:, n * nw:(n + 1) * nw] = (
            pbuf[n, h].astype(jnp.float32) + sib[n, 1].astype(jnp.float32)
            + xrecv[n].astype(jnp.float32)).astype(jnp.bfloat16)

    @pl.loop(0, groups)
    def _(g):
        for d in range(1, heads):
            a2a(g, d, h, lax.rem(h + d, heads)).wait_send()
        for k in range(last):
            @pl.when(jnp.logical_and(g >= AHEAD, jnp.logical_and(c < last, c >= k)))
            def _():
                up(g, k, c - k).wait_send()

            @pl.when(jnp.logical_and(g >= AHEAD, jnp.logical_and(c > 0, c + k <= last)))
            def _():
                down(g, k, c + k).wait_send()

        for b in range(ctxs):
            @pl.when(jnp.logical_and(g < merged, b < c))
            def _():
                for copy in part_down(g, b):
                    copy.wait_send()

            @pl.when(jnp.logical_and(g < merged, b > c))
            def _():
                for copy in part_up(g, b):
                    copy.wait_send()

    for d in range(1, ctxs):
        for g in range(AHEAD):
            gather(g, d, c, lax.rem(c + d, ctxs)).wait_send()
        for g in range(merged, groups):
            for copy in scatter(g, d, lax.rem(c + d, ctxs)):
                copy.wait_send()

    @pl.loop(0, ncols)
    def _(n):
        to_sibling(n, 0).wait_send()
        to_sibling(n, 1).wait_send()
        to_across(n).wait_send()


def fused_shards(ctxs, queries, keys, values, kept_rows, out_weight):
    rows, width = queries.shape
    key_count, hg = keys.shape
    cw = 2 * HD
    groups = hg // cw
    block = 4 * rows
    nw = 1024
    ncols = width // nw
    bf, f32 = jnp.bfloat16, jnp.float32
    dma = pltpu.SemaphoreType.DMA
    vmem = pl.BlockSpec(memory_space=pltpu.VMEM)
    hbm = pl.BlockSpec(memory_space=pl.ANY)
    return pl.pallas_call(
        kernel,
        out_shape=jax.ShapeDtypeStruct((rows, width), bf),
        in_specs=[hbm, hbm, hbm, pl.BlockSpec(memory_space=pltpu.SMEM), hbm],
        out_specs=vmem,
        scratch_shapes=[
            pltpu.VMEM((groups, key_count, cw), bf),
            pltpu.VMEM((groups, key_count, cw), bf),
            pltpu.VMEM((ncols, hg, nw), bf),
            pltpu.VMEM((groups, ctxs, block, cw), bf),
            pltpu.VMEM((groups, ctxs, block, cw), bf),
            pltpu.VMEM((groups, ctxs, 8, block), f32),
            pltpu.VMEM((DIRECT, ctxs - 1, block, cw), bf),
            pltpu.VMEM((DIRECT, ctxs - 1, 8, block), f32),
            pltpu.VMEM((groups, ctxs, block, cw), bf),
            pltpu.VMEM((groups, ctxs, 8, block), f32),
            pltpu.VMEM((groups, ctxs, block, cw), bf),
            pltpu.VMEM((groups, ctxs, 8, block), f32),
            pltpu.VMEM((8, key_count), f32),
            pltpu.VMEM((groups, block, cw), bf),
            pltpu.VMEM((ncols, 4, rows, nw), bf),
            pltpu.VMEM((ncols, 2, rows, nw), bf),
            pltpu.VMEM((ncols, rows, nw), bf),
            pltpu.VMEM((ncols, rows, nw), bf),
            pltpu.VMEM((2, 2 * block, key_count), f32),
            pltpu.VMEM((2, 2 * block, key_count), bf),
            pltpu.VMEM((2, 2 * block, HD), f32),
            pltpu.VMEM((ncols, block, nw), f32),
            dma((2, groups)), dma((ncols,)), dma((groups,)),
            dma((groups, ctxs - 1)), dma((groups, ctxs - 1)),
            dma((groups, ctxs - 1)), dma((groups, ctxs - 1)),
            dma((groups, 3)), dma((groups, 3)),
            dma((AHEAD, ctxs - 1)), dma((AHEAD, ctxs - 1)),
            dma((DIRECT, ctxs - 1)), dma((DIRECT, ctxs - 1)),
            dma((DIRECT, ctxs - 1)), dma((DIRECT, ctxs - 1)),
            dma((2, groups, ctxs)), dma((2, groups, ctxs)),
            dma((2, groups, ctxs)), dma((2, groups, ctxs)),
            dma((ncols, 2)), dma((ncols, 2)),
            dma((ncols,)), dma((ncols,)),
        ],
        compiler_params=pltpu.CompilerParams(
            collective_id=0, has_side_effects=True, vmem_limit_bytes=62 * 2**20),
        cost_estimate=pl.CostEstimate(
            flops=4 * ctxs * block * key_count * hg + 2 * block * hg * width,
            bytes_accessed=2 * (2 * key_count * hg + hg * width),
            transcendentals=ctxs * block * key_count * hg // HD),
        name="attention",
    )(queries, keys, values, kept_rows, out_weight)


def solution(mesh):
    heads, ctxs = mesh.shape["head"], mesh.shape["ctx"]

    def shards(queries, keys, values, kept_rows, out_weight):
        rows = queries.shape[0]
        if heads == 4 and ctxs == 4 and rows == 32 and keys.shape[1] == 12 * HD:
            return fused_shards(ctxs, queries, keys, values, kept_rows, out_weight)
        return general_shards(queries, keys, values, kept_rows, out_weight)

    placed = (
        P(("abl", "head", "ctx"), None),
        P(("abl", "ctx"), "head"),
        P(("abl", "ctx"), "head"),
        P(("abl", "ctx")),
        P("head", None),
    )
    return jax.shard_map(
        shards,
        mesh=mesh,
        in_specs=placed,
        out_specs=P(("abl", "head", "ctx"), None),
        check_vma=False,
    )
```
